128 devices in a mesh: lat: 32 (over y, x_lo, z), lon: 2 (over core), ens: 2 (over x_hi).
Axes of the slice: x: 4 (x_hi: 2, x_lo: 2; x = x_hi * 2 + x_lo), y: 4, z: 4, core: 2. Of those that a mesh axis runs over, the one named last changes fastest.
Arguments:
- fields: bfloat16 [2, 64, 1440, 256], P('ens', 'lat', 'lon'), may hold values from -6 to 6
- cotangent: bfloat16 [2, 64, 1440, 256], P('ens', 'lat', 'lon'), may hold values from -6 to 6
- weights: bfloat16 [9, 256, 32], replicated, may hold values from -0.375 to 0.375
- basis_values: bfloat16 [64, 5, 9, 5], replicated, may hold values from 0 to 0.5
- support: int32 [64, 5], replicated, may hold values from -2 to 65, as said below
- counts: int32 [64], replicated, may hold values from 1 to 5, as said below
Outputs:
- mixed_output: bfloat16 [2, 64, 1440, 256], P('ens', 'lat', 'lon')
- input_grad: bfloat16 [2, 64, 1440, 256], P('ens', 'lat', 'lon')
- weight_grad: float32 [9, 256, 32], P(None, 'lat')
The draws below stay inside these ranges and needn't reach their ends.
Inputs may be any that keep to these rules, and one draw needn't show every extreme that they name: `support`: the first counts[i] entries of row i are consecutive increasing virtual rows, each within 2 of i; later entries equal i. Row 0 holds -2 and row 63 holds 65. `counts`: rows 0 and 63 use all slots.
All inputs are finite; a program needn't handle non-finite values.
Results may differ from the reference program's by a relative error of at most 0.005.
Values may be sent and summed in bfloat16 or wider, within the bound.
A program may use at most 256 MiB of HBM per device.

```python
import math
import jax
import jax.numpy as jnp
from jax import lax

C = 256
GW = 32
K = 9
NLON = 1440
HDEPTH = 2
HW = 2
SMAX = 5
WIN = 5
NLAT = 64
MEMBERS = 2


def support_law(key):
    count_key, start_key = jax.random.split(jax.random.fold_in(key, 7))
    row_ids = jnp.arange(NLAT, dtype=jnp.int32)
    live_counts = jax.random.randint(count_key, (NLAT,), 1, SMAX + 1).astype(jnp.int32)
    live_counts = live_counts.at[1].set(1)
    live_counts = live_counts.at[0].set(SMAX)
    live_counts = live_counts.at[NLAT - 1].set(SMAX)
    offsets = jax.random.randint(start_key, (NLAT,), 0, SMAX - live_counts + 1).astype(jnp.int32)
    slot_ids = jnp.arange(SMAX, dtype=jnp.int32)
    rows_out = row_ids[:, None] - HDEPTH + offsets[:, None] + slot_ids[None, :]
    rows_out = jnp.where(slot_ids[None, :] < live_counts[:, None], rows_out, row_ids[:, None])
    return (rows_out.astype(jnp.int32), live_counts)


def draw_support(key, part):
    return support_law(key)[0]


def draw_counts(key, part):
    return support_law(key)[1]


def level_of(rng, shape, shards, low, high):
    level, own = 1.0, jax.random.fold_in(rng, 6)
    for axis_at, shards_of in shards:
        heights = jnp.exp(jax.random.uniform(jax.random.fold_in(own, axis_at), (shards_of,), jnp.float32, low / len(shards), high / len(shards)))
        level = level * jnp.repeat(heights, shape[axis_at] // shards_of).reshape([-1 if axis == axis_at else 1 for axis in range(len(shape))])
    return level


def gaussian(rng, dims, deviation, limit, cuts=(), kind=jnp.bfloat16):
    loudness = level_of(rng, dims, cuts, -0.22, 0.18) if cuts else 1.0
    result = jax.random.normal(rng, dims, jnp.float32) * deviation * loudness
    return jnp.minimum(jnp.maximum(result, -limit), limit).astype(kind)


def setup_inputs(seed: int = 0) -> dict:
    splits = jax.random.split(jax.random.key(seed), 7)
    return {
        "fields": gaussian(splits[0], (MEMBERS, NLAT, NLON, C), 1.0, 6.0, ((0, 2), (1, 32), (2, 2))),
        "cotangent": gaussian(splits[1], (MEMBERS, NLAT, NLON, C), 1.0, 6.0, ((0, 2), (1, 32), (2, 2))),
        "weights": gaussian(splits[2], (K, C, GW), (K * GW) ** -0.5, 0.375),
        "basis_values": jnp.clip(jax.random.uniform(splits[3], (NLAT, SMAX, K, WIN), jnp.float32, 0.0, 0.5), 0.0, 0.5).astype(jnp.bfloat16),
        "support": draw_support(jax.random.fold_in(splits[6], 71), 0),
        "counts": draw_counts(jax.random.fold_in(splits[6], 71), 0),
    }


def kernel_rows(basis_rows, count_rows, weights):
    slot_ids = jnp.arange(basis_rows.shape[1], dtype=jnp.int32)
    alive_mask = (slot_ids[None, :] < count_rows[:, None]).astype(jnp.float32)
    masked = basis_rows.astype(jnp.float32) * alive_mask[:, :, None, None]
    mixing = weights.astype(jnp.float32).reshape(weights.shape[0], weights.shape[1] // weights.shape[2], weights.shape[2], weights.shape[2])
    combined = jnp.einsum('uskm,kgoc->usmgco', masked, mixing, precision=lax.Precision.HIGHEST)
    return (masked, combined.astype(jnp.bfloat16))

def virtual_field(field_rows):
    half_turn = NLON // 2
    north_rows = jnp.roll(jnp.flip(field_rows[:HDEPTH], 0), half_turn, axis=1)
    south_rows = jnp.roll(jnp.flip(field_rows[NLAT - HDEPTH:], 0), half_turn, axis=1)
    stacked = jnp.concatenate([north_rows, field_rows, south_rows], axis=0)
    return jnp.concatenate([stacked[:, NLON - HW:], stacked, stacked[:, :HW]], axis=1)

def reference(fields, cotangent, weights, basis_values, support, counts):
    groups = C // GW
    grad_scale = 1.0 / math.sqrt(NLAT * NLON * MEMBERS)
    masked_all, combined_all = kernel_rows(basis_values, counts, weights)
    outputs = []
    input_grads = []
    weight_acc = jnp.zeros((K, groups, GW, GW), jnp.float32)
    half_turn = NLON // 2
    for member_index in range(MEMBERS):
        padded = virtual_field(fields[member_index])
        grad_member = cotangent[member_index]
        grad_padded = jnp.concatenate([grad_member[:, NLON - HW:], grad_member, grad_member[:, :HW]], axis=1)

        def forward_row(row_index):
            picked_rows = padded[support[row_index] + HDEPTH]
            windows = jnp.stack([picked_rows[:, shift_index:shift_index + NLON] for shift_index in range(WIN)], axis=2)
            windows = windows.reshape(SMAX, NLON, WIN, groups, GW).astype(jnp.float32)
            kernel = combined_all[row_index].astype(jnp.float32)
            out_row = jnp.einsum('sjmgc,smgco->jgo', windows, kernel, precision=lax.Precision.HIGHEST)
            grad_out = grad_member[row_index].reshape(NLON, groups, GW).astype(jnp.float32)
            kernel_grad = jnp.einsum('sjmgc,jgo->smgco', windows, grad_out, precision=lax.Precision.HIGHEST)
            weight_part = jnp.einsum('skm,smgco->kgoc', masked_all[row_index], kernel_grad, precision=lax.Precision.HIGHEST)
            return (out_row.reshape(NLON, C).astype(jnp.bfloat16), weight_part)
        out_rows, weight_parts = lax.map(forward_row, jnp.arange(NLAT, dtype=jnp.int32))
        weight_acc = weight_acc + lax.optimization_barrier(jnp.sum(weight_parts, axis=0))
        outputs.append(out_rows)

        def adjoint_row(row_index, buffer):
            grad_rows = grad_padded[row_index]
            windows = jnp.stack([grad_rows[2 * HW - shift_index:2 * HW - shift_index + NLON] for shift_index in range(WIN)], axis=1)
            windows = windows.reshape(NLON, WIN, groups, GW).astype(jnp.float32)
            kernel = combined_all[row_index].astype(jnp.float32)
            contrib = jnp.einsum('jmgo,smgco->sjgc', windows, kernel, precision=lax.Precision.HIGHEST).reshape(SMAX, NLON, C)
            return buffer.at[(support[row_index] + HDEPTH).astype(jnp.int32)].add(contrib)
        buffer = lax.fori_loop(0, NLAT, adjoint_row, jnp.zeros((NLAT + 2 * HDEPTH, NLON, C), jnp.float32))
        grad_field = buffer[HDEPTH:HDEPTH + NLAT]
        north_rows = jnp.roll(jnp.flip(buffer[:HDEPTH], 0), half_turn, axis=1)
        south_rows = jnp.roll(jnp.flip(buffer[HDEPTH + NLAT:], 0), half_turn, axis=1)
        grad_field = grad_field.at[:HDEPTH].add(north_rows)
        grad_field = grad_field.at[NLAT - HDEPTH:].add(south_rows)
        input_grads.append(grad_field.astype(jnp.bfloat16))
    weight_grad = (weight_acc * grad_scale).reshape(K, C, GW)
    return (jnp.stack(outputs, axis=0), jnp.stack(input_grads, axis=0), weight_grad)
```

```python
import functools
import math

import jax
import jax.numpy as jnp
from jax import lax
from jax.experimental import pallas as pl
from jax.experimental.pallas import tpu as pltpu
from jax.sharding import PartitionSpec as P

MESH = pl.DeviceIdType.MESH
BF16 = jnp.bfloat16
F32 = jnp.float32

C = 256
GW = 32
K = 9
SMAX = 5
WIN = 5
PAD = 16
LW = 128
NB = C // LW
PB = LW // GW
PANEL = 6
TAPS = PANEL * WIN * LW


def chunks_of(cols):
    starts = list(range(0, cols, 256))
    if len(starts) > 1 and cols - starts[-1] < 32:
        starts.pop()
    compute = [(s, (starts[j + 1] if j + 1 < len(starts) else cols) - s) for j, s in enumerate(starts)]
    cuts = [0] + [s + 16 for s in starts[1:]] + [cols]
    send = [(cuts[j], cuts[j + 1] - cuts[j]) for j in range(len(starts))]
    return compute, send


def body(
    lat_n,
    cols,
    fields,
    cot,
    wf,
    wa,
    basis,
    support,
    counts,
    out,
    grad,
    wout,
    xp,
    cp,
    xs,
    cs,
    kf,
    ka,
    cw,
    xt,
    win,
    gbuf,
    tab,
    own_sem,
    row_send,
    row_recv,
    edge_send,
    edge_recv,
):
    compute, send = chunks_of(cols)
    kcols = cw.shape[2]
    lat = lax.axis_index("lat")
    lon = lax.axis_index("lon")
    ens = lax.axis_index("ens")
    sib = 1 - lon
    nlat = lat_n * 2
    top = lat == 0
    bottom = lat == lat_n - 1
    sources = (fields, cot)
    panels = (xp, cp)
    wides = (xs, cs)

    barrier = pltpu.get_barrier_semaphore()
    pl.semaphore_signal(barrier, inc=1, device_id=(lat, sib, ens), device_id_type=MESH)

    @pl.when(jnp.logical_not(top))
    def _():
        for to in (lon, sib):
            pl.semaphore_signal(barrier, inc=1, device_id=(lat - 1, to, ens), device_id_type=MESH)

    @pl.when(jnp.logical_not(bottom))
    def _():
        for to in (lon, sib):
            pl.semaphore_signal(barrier, inc=1, device_id=(lat + 1, to, ens), device_id_type=MESH)

    pl.semaphore_wait(barrier, 5 - 2 * jnp.where(top, 1, 0) - 2 * jnp.where(bottom, 1, 0))

    def own_copy(t, a):
        return pltpu.make_async_copy(
            sources[t].at[a], panels[t].at[2 + a, pl.ds(PAD, cols)], own_sem.at[t, a]
        )

    def target(dirn, a):
        if dirn == 0:
            return (
                jnp.where(top, 0, lat - 1),
                jnp.where(top, sib, lon),
                jnp.where(top, 1 - a, 4 + a),
            )
        return (
            jnp.where(bottom, lat, lat + 1),
            jnp.where(bottom, sib, lon),
            jnp.where(bottom, 5 - a, a),
        )

    def row_copy(t, dirn, a, ch):
        to_lat, to_lon, slot = target(dirn, a)
        start, size = send[ch]
        return pltpu.make_async_remote_copy(
            src_ref=sources[t].at[a, pl.ds(start, size)],
            dst_ref=panels[t].at[slot, pl.ds(PAD + start, size)],
            send_sem=row_send.at[t, dirn, a, ch],
            recv_sem=row_recv.at[t, slot, ch],
            device_id=(to_lat, to_lon, ens),
            device_id_type=MESH,
        )

    def edge_refs(t, a, slot, side):
        src = sources[t].at[a, pl.ds(cols - PAD if side == 0 else 0, PAD)]
        dst = panels[t].at[slot, pl.ds(0 if side == 0 else PAD + cols, PAD)]
        return src, dst

    def edge_copy(t, where_to, a, slot, side, to_lat, to_lon):
        src, dst = edge_refs(t, a, slot, side)
        return pltpu.make_async_remote_copy(
            src_ref=src,
            dst_ref=dst,
            send_sem=edge_send.at[t, where_to, a, side],
            recv_sem=edge_recv.at[t, slot, side],
            device_id=(to_lat, to_lon, ens),
            device_id_type=MESH,
        )

    def edges(t):
        for a in range(2):
            for side in range(2):
                edge_copy(t, 2, a, 2 + a, side, lat, sib).start()
        for dirn, pole in ((0, top), (1, bottom)):
            for a in range(2):
                to_lat, _, slot = target(dirn, a)
                for side in range(2):

                    @pl.when(pole)
                    def _():
                        src, dst = edge_refs(t, a, slot, side)
                        pltpu.make_async_copy(src, dst, edge_recv.at[t, slot, side]).start()

                    @pl.when(jnp.logical_not(pole))
                    def _():
                        edge_copy(t, dirn, a, slot, side, to_lat, sib).start()

    def edges_sent(t):
        for a in range(2):
            for side in range(2):
                edge_copy(t, 2, a, 2 + a, side, lat, sib).wait_send()
        for dirn, pole in ((0, top), (1, bottom)):
            for a in range(2):
                to_lat, _, slot = target(dirn, a)
                for side in range(2):

                    @pl.when(jnp.logical_not(pole))
                    def _():
                        edge_copy(t, dirn, a, slot, side, to_lat, sib).wait_send()

    def wait_edge(t, slot):
        for side in range(2):
            src, dst = edge_refs(t, 0, slot, side)
            pltpu.make_async_copy(dst, dst, edge_recv.at[t, slot, side]).wait()

    def wait_row(t, slot, ch):
        start, size = send[ch]
        dst = panels[t].at[slot, pl.ds(PAD + start, size)]
        pltpu.make_async_copy(dst, dst, row_recv.at[t, slot, ch]).wait()

    for t in range(2):
        for a in range(2):
            own_copy(t, a).start()
    for t in range(2):
        edges(t)
        for ch in range(len(send)):
            for dirn in range(2):
                for a in range(2):
                    row_copy(t, dirn, a, ch).start()

    group_of = lax.broadcasted_iota(jnp.int32, (GW, LW), 1) // GW

    def row_of(virtual):
        mirrored = jnp.logical_or(virtual < 0, virtual >= nlat)
        real = jnp.where(
            virtual < 0, -1 - virtual, jnp.where(virtual >= nlat, 2 * nlat - 1 - virtual, virtual)
        )
        return real, mirrored

    def coefficients(real, offset):
        first = support[real * SMAX] - real
        slot = offset - first
        live = jnp.logical_and(slot >= 0, slot < counts[real])
        slot = jnp.minimum(jnp.maximum(slot, 0), SMAX - 1)
        base = (real * SMAX + slot) * (K * WIN)
        gate = jnp.where(live, 1.0, 0.0).astype(F32)
        return [[basis[base + k * WIN + m] * gate for m in range(WIN)] for k in range(K)]

    def spread(kref, wref, a, p, coef):
        for m0, m1 in ((0, 3), (3, 5)):
            sums = [jnp.zeros((GW, C), F32) for _ in range(m0, m1)]
            for k in range(K):
                wk = wref[k]
                for m in range(m0, m1):
                    sums[m - m0] = sums[m - m0] + coef[k][m] * wk
            for m in range(m0, m1):
                for b in range(NB):
                    part = sums[m - m0][:, b * LW : (b + 1) * LW]
                    for q in range(PB):
                        row = pl.multiple_of(p * (WIN * LW) + m * LW + q * GW, GW)
                        kref[b, pl.ds(row, GW), a * LW : (a + 1) * LW] = jnp.where(
                            group_of == q, part, 0.0
                        ).astype(BF16)

    for a in range(2):
        def forward_offset(q, carry):
            coef = coefficients(lat * 2 + a, q - 2)
            for k in range(K):
                for m in range(WIN):
                    tab[(a * SMAX + q) * (K * WIN) + k * WIN + m] = coef[k][m]
            spread(kf, wf, a, a + q, coef)
            return carry

        def adjoint_offset(q, carry):
            real, mirrored = row_of(lat * 2 - 2 + a + q)
            coef = coefficients(real, jnp.where(mirrored, q - 2, 2 - q))
            spread(ka, wa, a, a + q, coef)
            return carry

        lax.fori_loop(0, SMAX, forward_offset, 0)
        lax.fori_loop(0, SMAX, adjoint_offset, 0)
    for kref in (kf, ka):
        for b in range(NB):
            kref[b, 5 * WIN * LW :, 0:LW] = jnp.zeros((WIN * LW, LW), BF16)
            kref[b, 0 : WIN * LW, LW : 2 * LW] = jnp.zeros((WIN * LW, LW), BF16)

    def widen(t, slot, start, size):
        for b in range(NB):
            wides[t][b, slot, start : start + size, :] = panels[t][
                slot, start : start + size, b * LW : (b + 1) * LW
            ].astype(F32)

    for t in range(2):
        for a in range(2):
            own_copy(t, a).wait()
            wait_edge(t, 2 + a)
            widen(t, 2 + a, 0, cols + 2 * PAD)

    def own_windows(b, carry):
        for m in range(WIN):
            for a in range(2):
                cw[b, m, 0:cols, a * LW : (a + 1) * LW] = cs[
                    b, 2 + a, PAD + 2 - m : PAD + 2 - m + cols, :
                ].astype(BF16)
            if kcols > cols:
                cw[b, m, cols:kcols, :] = jnp.zeros((kcols - cols, 2 * LW), BF16)
        return carry

    lax.fori_loop(0, NB, own_windows, 0)

    def convolve(t, ch, kref, dest, sign):
        start, size = compute[ch]
        for b in range(NB):

            def window_row(p, carry):
                for m in range(WIN):
                    shift = PAD + start + sign * (m - 2)
                    lane = pl.multiple_of(p * (WIN * LW) + m * LW, LW)
                    win[0:size, pl.ds(lane, LW)] = wides[t][
                        b, p, shift : shift + size, :
                    ].astype(BF16)
                return carry

            lax.fori_loop(0, PANEL, window_row, 0)
            res = jnp.dot(win[0:size, :], kref[b], preferred_element_type=F32)
            for a in range(2):
                dest[a, start : start + size, b * LW : (b + 1) * LW] = res[
                    :, a * LW : (a + 1) * LW
                ].astype(BF16)

    def arrive(t, ch):
        start, size = send[ch]
        for slot in (0, 1, 4, 5):
            if ch == 0:
                wait_edge(t, slot)
            wait_row(t, slot, ch)
            lo = 0 if ch == 0 else PAD + start
            hi = PAD + start + size + (PAD if ch == len(send) - 1 else 0)
            widen(t, slot, lo, hi - lo)

    for ch in range(len(compute)):
        arrive(0, ch)
        convolve(0, ch, kf, out, 1)

    def transpose_row(slot, carry):
        for b in range(NB):
            row = pl.multiple_of(slot * LW, LW)
            xt[b, pl.ds(row, LW), 0:cols] = xs[b, slot, PAD : PAD + cols, :].T.astype(BF16)
            if kcols > cols:
                xt[b, pl.ds(row, LW), cols:kcols] = jnp.zeros((LW, kcols - cols), BF16)
        return carry

    lax.fori_loop(0, PANEL, transpose_row, 0)
    wout[...] = jnp.zeros(wout.shape, F32)
    for b in range(NB):

        def weight_offset(m, carry):
            gbuf[...] = jnp.dot(xt[b], cw[b, m], preferred_element_type=F32)
            sums = [wout[k * GW : (k + 1) * GW, b * LW : (b + 1) * LW] for k in range(K)]
            for a in range(2):
                for q in range(SMAX):
                    low = (a + q) * LW
                    part = gbuf[low : low + GW, a * LW : (a + 1) * LW]
                    for g in range(1, PB):
                        part = jnp.where(
                            group_of == g,
                            gbuf[low + g * GW : low + (g + 1) * GW, a * LW : (a + 1) * LW],
                            part,
                        )
                    for k in range(K):
                        sums[k] = sums[k] + tab[(a * SMAX + q) * (K * WIN) + k * WIN + m] * part
            for k in range(K):
                wout[k * GW : (k + 1) * GW, b * LW : (b + 1) * LW] = sums[k]
            return carry

        lax.fori_loop(0, WIN, weight_offset, 0)

    for ch in range(len(compute)):
        arrive(1, ch)
        convolve(1, ch, ka, grad, -1)

    for t in range(2):
        edges_sent(t)
        for ch in range(len(send)):
            for dirn in range(2):
                for a in range(2):
                    row_copy(t, dirn, a, ch).wait_send()


def shards(fields, cotangent, weights, basis_values, support, counts):
    lat_n = lax.axis_size("lat")
    lat = lax.axis_index("lat")
    cols = fields.shape[2]
    kcols = -(-cols // 128) * 128
    n_chunks = len(chunks_of(cols)[0])
    w4 = weights.astype(F32).reshape(K, C // GW, GW, GW)
    wf = jnp.transpose(w4, (0, 3, 1, 2)).reshape(K, GW, C)
    wa = jnp.transpose(w4, (0, 2, 1, 3)).reshape(K, GW, C)
    vmem = pl.BlockSpec(memory_space=pltpu.VMEM)
    smem = pl.BlockSpec(memory_space=pltpu.SMEM)
    hbm = pl.BlockSpec(memory_space=pl.ANY)
    dma = pltpu.SemaphoreType.DMA
    out, grad, wsum = pl.pallas_call(
        functools.partial(body, lat_n, cols),
        out_shape=(
            jax.ShapeDtypeStruct((2, cols, C), BF16),
            jax.ShapeDtypeStruct((2, cols, C), BF16),
            jax.ShapeDtypeStruct((K * GW, C), F32),
        ),
        in_specs=[hbm, hbm, vmem, vmem, smem, smem, smem],
        out_specs=(vmem, vmem, vmem),
        scratch_shapes=[
            pltpu.VMEM((PANEL, cols + 2 * PAD, C), BF16),
            pltpu.VMEM((PANEL, cols + 2 * PAD, C), BF16),
            pltpu.VMEM((NB, PANEL, cols + 2 * PAD, LW), F32),
            pltpu.VMEM((NB, PANEL, cols + 2 * PAD, LW), F32),
            pltpu.VMEM((NB, TAPS, 2 * LW), BF16),
            pltpu.VMEM((NB, TAPS, 2 * LW), BF16),
            pltpu.VMEM((NB, WIN, kcols, 2 * LW), BF16),
            pltpu.VMEM((NB, PANEL * LW, kcols), BF16),
            pltpu.VMEM((256, TAPS), BF16),
            pltpu.VMEM((PANEL * LW, 2 * LW), F32),
            pltpu.SMEM((2 * SMAX * K * WIN,), F32),
            dma((2, 2)),
            dma((2, 2, 2, n_chunks)),
            dma((2, PANEL, n_chunks)),
            dma((2, 3, 2, 2)),
            dma((2, PANEL, 2)),
        ],
        compiler_params=pltpu.CompilerParams(
            collective_id=0, has_side_effects=True, vmem_limit_bytes=56 * 1024 * 1024
        ),
        name="disco",
    )(
        fields[0],
        cotangent[0],
        wf,
        wa,
        basis_values.astype(F32).reshape(-1),
        support.reshape(-1),
        counts,
    )
    total = 2 * lat_n * cols * lax.axis_size("lon") * lax.axis_size("ens") * fields.shape[0]
    wsum = lax.psum(wsum * (1.0 / math.sqrt(total)), ("lat", "lon", "ens")).reshape(K, GW, C)
    share = C // lat_n
    mine = lax.dynamic_slice_in_dim(wsum, lat * share, share, 2)
    return (out[None], grad[None], jnp.transpose(mine, (0, 2, 1)))


def solution(mesh):
    placed = (P("ens", "lat", "lon", None), P("ens", "lat", "lon", None), P(), P(), P(), P())
    return jax.shard_map(
        shards,
        mesh=mesh,
        in_specs=placed,
        out_specs=(
            P("ens", "lat", "lon", None),
            P("ens", "lat", "lon", None),
            P(None, "lat", None),
        ),
        check_vma=False,
    )
```

```python
import functools
import math

import jax
import jax.numpy as jnp
from jax import lax
from jax.experimental import pallas as pl
from jax.experimental.pallas import tpu as pltpu
from jax.sharding import PartitionSpec as P

MESH = pl.DeviceIdType.MESH
BF16 = jnp.bfloat16
F32 = jnp.float32

C = 256
GW = 32
K = 9
SMAX = 5
WIN = 5
PAD = 16
LW = 128
NB = C // LW
PB = LW // GW
PANEL = 6
TAPS = PANEL * WIN * LW


def chunks_of(cols):
    starts = list(range(0, cols, 256))
    if len(starts) > 1 and cols - starts[-1] < 32:
        starts.pop()
    compute = [(s, (starts[j + 1] if j + 1 < len(starts) else cols) - s) for j, s in enumerate(starts)]
    cuts = [0] + [s + 16 for s in starts[1:]] + [cols]
    send = [(cuts[j], cuts[j + 1] - cuts[j]) for j in range(len(starts))]
    return compute, send


def body(
    lat_n,
    cols,
    scale,
    fields,
    cot,
    wf,
    wa,
    basis,
    support,
    counts,
    out,
    grad,
    wout,
    xp,
    cp,
    xs,
    cs,
    kf,
    ka,
    cw,
    xt,
    win,
    gbuf,
    tab,
    wacc,
    wt,
    half,
    quarter,
    shares,
    final,
    own_sem,
    row_send,
    row_recv,
    edge_send,
    edge_recv,
    sum_send,
    sum_recv,
    share_send,
    share_recv,
    final_send,
    final_recv,
):
    compute, send = chunks_of(cols)
    kcols = cw.shape[2]
    lat = lax.axis_index("lat")
    lon = lax.axis_index("lon")
    ens = lax.axis_index("ens")
    sib = 1 - lon
    nlat = lat_n * 2
    top = lat == 0
    bottom = lat == lat_n - 1
    sources = (fields, cot)
    panels = (xp, cp)
    wides = (xs, cs)

    barrier = pltpu.get_barrier_semaphore()
    pl.semaphore_signal(barrier, inc=1, device_id=(lat, sib, ens), device_id_type=MESH)

    @pl.when(jnp.logical_not(top))
    def _():
        for to in (lon, sib):
            pl.semaphore_signal(barrier, inc=1, device_id=(lat - 1, to, ens), device_id_type=MESH)

    @pl.when(jnp.logical_not(bottom))
    def _():
        for to in (lon, sib):
            pl.semaphore_signal(barrier, inc=1, device_id=(lat + 1, to, ens), device_id_type=MESH)

    mine = lon * 2 + ens
    n_shares = lat_n // 4
    share = C // lat_n
    owner = lax.rem(lat // 8 + lat, 4) == mine
    partners = ((sib, ens), (lon, 1 - ens), (sib, 1 - ens))

    def share_lat(j):
        return 4 * j + lax.rem(mine - j // 2 + 4 * lat_n, 4)

    for to_lon, to_ens in partners[1:]:
        pl.semaphore_signal(barrier, inc=1, device_id=(lat, to_lon, to_ens), device_id_type=MESH)

    @pl.when(owner)
    def _():
        def greet(j, carry):
            pl.semaphore_signal(
                barrier, inc=1, device_id=(j + jnp.where(j < lat, 0, 1), lon, ens), device_id_type=MESH
            )
            return carry

        lax.fori_loop(0, lat_n - 1, greet, 0)

    pl.semaphore_wait(
        barrier,
        7
        + n_shares
        - jnp.where(owner, 1, 0)
        - 2 * jnp.where(top, 1, 0)
        - 2 * jnp.where(bottom, 1, 0),
    )

    def own_copy(t, a):
        return pltpu.make_async_copy(
            sources[t].at[a], panels[t].at[2 + a, pl.ds(PAD, cols)], own_sem.at[t, a]
        )

    def target(dirn, a):
        if dirn == 0:
            return (
                jnp.where(top, 0, lat - 1),
                jnp.where(top, sib, lon),
                jnp.where(top, 1 - a, 4 + a),
            )
        return (
            jnp.where(bottom, lat, lat + 1),
            jnp.where(bottom, sib, lon),
            jnp.where(bottom, 5 - a, a),
        )

    def row_copy(t, dirn, a, ch):
        to_lat, to_lon, slot = target(dirn, a)
        start, size = send[ch]
        return pltpu.make_async_remote_copy(
            src_ref=sources[t].at[a, pl.ds(start, size)],
            dst_ref=panels[t].at[slot, pl.ds(PAD + start, size)],
            send_sem=row_send.at[t, dirn, a, ch],
            recv_sem=row_recv.at[t, slot, ch],
            device_id=(to_lat, to_lon, ens),
            device_id_type=MESH,
        )

    def edge_refs(t, a, slot, side):
        src = sources[t].at[a, pl.ds(cols - PAD if side == 0 else 0, PAD)]
        dst = panels[t].at[slot, pl.ds(0 if side == 0 else PAD + cols, PAD)]
        return src, dst

    def edge_copy(t, where_to, a, slot, side, to_lat, to_lon):
        src, dst = edge_refs(t, a, slot, side)
        return pltpu.make_async_remote_copy(
            src_ref=src,
            dst_ref=dst,
            send_sem=edge_send.at[t, where_to, a, side],
            recv_sem=edge_recv.at[t, slot, side],
            device_id=(to_lat, to_lon, ens),
            device_id_type=MESH,
        )

    def edges(t):
        for a in range(2):
            for side in range(2):
                edge_copy(t, 2, a, 2 + a, side, lat, sib).start()
        for dirn, pole in ((0, top), (1, bottom)):
            for a in range(2):
                to_lat, _, slot = target(dirn, a)
                for side in range(2):

                    @pl.when(pole)
                    def _():
                        src, dst = edge_refs(t, a, slot, side)
                        pltpu.make_async_copy(src, dst, edge_recv.at[t, slot, side]).start()

                    @pl.when(jnp.logical_not(pole))
                    def _():
                        edge_copy(t, dirn, a, slot, side, to_lat, sib).start()

    def edges_sent(t):
        for a in range(2):
            for side in range(2):
                edge_copy(t, 2, a, 2 + a, side, lat, sib).wait_send()
        for dirn, pole in ((0, top), (1, bottom)):
            for a in range(2):
                to_lat, _, slot = target(dirn, a)
                for side in range(2):

                    @pl.when(jnp.logical_not(pole))
                    def _():
                        edge_copy(t, dirn, a, slot, side, to_lat, sib).wait_send()

    def wait_edge(t, slot):
        for side in range(2):
            src, dst = edge_refs(t, 0, slot, side)
            pltpu.make_async_copy(dst, dst, edge_recv.at[t, slot, side]).wait()

    def wait_row(t, slot, ch):
        start, size = send[ch]
        dst = panels[t].at[slot, pl.ds(PAD + start, size)]
        pltpu.make_async_copy(dst, dst, row_recv.at[t, slot, ch]).wait()

    for t in range(2):
        for a in range(2):
            own_copy(t, a).start()
    for t in range(2):
        edges(t)
        for ch in range(len(send)):
            for dirn in range(2):
                for a in range(2):
                    row_copy(t, dirn, a, ch).start()

    group_of = lax.broadcasted_iota(jnp.int32, (GW, LW), 1) // GW

    def row_of(virtual):
        mirrored = jnp.logical_or(virtual < 0, virtual >= nlat)
        real = jnp.where(
            virtual < 0, -1 - virtual, jnp.where(virtual >= nlat, 2 * nlat - 1 - virtual, virtual)
        )
        return real, mirrored

    def coefficients(real, offset):
        first = support[real * SMAX] - real
        slot = offset - first
        live = jnp.logical_and(slot >= 0, slot < counts[real])
        slot = jnp.minimum(jnp.maximum(slot, 0), SMAX - 1)
        base = (real * SMAX + slot) * (K * WIN)
        gate = jnp.where(live, 1.0, 0.0).astype(F32)
        return [[basis[base + k * WIN + m] * gate for m in range(WIN)] for k in range(K)]

    def spread(kref, wref, a, p, coef):
        for m0, m1 in ((0, 3), (3, 5)):
            sums = [jnp.zeros((GW, C), F32) for _ in range(m0, m1)]
            for k in range(K):
                wk = wref[k]
                for m in range(m0, m1):
                    sums[m - m0] = sums[m - m0] + coef[k][m] * wk
            for m in range(m0, m1):
                for b in range(NB):
                    part = sums[m - m0][:, b * LW : (b + 1) * LW]
                    for q in range(PB):
                        row = pl.multiple_of(p * (WIN * LW) + m * LW + q * GW, GW)
                        kref[b, pl.ds(row, GW), a * LW : (a + 1) * LW] = jnp.where(
                            group_of == q, part, 0.0
                        ).astype(BF16)

    for a in range(2):
        def forward_offset(q, carry):
            coef = coefficients(lat * 2 + a, q - 2)
            for k in range(K):
                for m in range(WIN):
                    tab[(a * SMAX + q) * (K * WIN) + k * WIN + m] = coef[k][m]
            spread(kf, wf, a, a + q, coef)
            return carry

        def adjoint_offset(q, carry):
            real, mirrored = row_of(lat * 2 - 2 + a + q)
            coef = coefficients(real, jnp.where(mirrored, q - 2, 2 - q))
            spread(ka, wa, a, a + q, coef)
            return carry

        lax.fori_loop(0, SMAX, forward_offset, 0)
        lax.fori_loop(0, SMAX, adjoint_offset, 0)
    for kref in (kf, ka):
        for b in range(NB):
            kref[b, 5 * WIN * LW :, 0:LW] = jnp.zeros((WIN * LW, LW), BF16)
            kref[b, 0 : WIN * LW, LW : 2 * LW] = jnp.zeros((WIN * LW, LW), BF16)

    def widen(t, slot, start, size):
        for b in range(NB):
            wides[t][b, slot, start : start + size, :] = panels[t][
                slot, start : start + size, b * LW : (b + 1) * LW
            ].astype(F32)

    for t in range(2):
        for a in range(2):
            own_copy(t, a).wait()
            wait_edge(t, 2 + a)
            widen(t, 2 + a, 0, cols + 2 * PAD)

    def own_windows(b, carry):
        for m in range(WIN):
            for a in range(2):
                cw[b, m, 0:cols, a * LW : (a + 1) * LW] = cs[
                    b, 2 + a, PAD + 2 - m : PAD + 2 - m + cols, :
                ].astype(BF16)
            if kcols > cols:
                cw[b, m, cols:kcols, :] = jnp.zeros((kcols - cols, 2 * LW), BF16)
        return carry

    lax.fori_loop(0, NB, own_windows, 0)

    def convolve(t, ch, kref, dest, sign):
        start, size = compute[ch]
        for b in range(NB):

            def window_row(p, carry):
                for m in range(WIN):
                    shift = PAD + start + sign * (m - 2)
                    lane = pl.multiple_of(p * (WIN * LW) + m * LW, LW)
                    win[0:size, pl.ds(lane, LW)] = wides[t][
                        b, p, shift : shift + size, :
                    ].astype(BF16)
                return carry

            lax.fori_loop(0, PANEL, window_row, 0)
            res = jnp.dot(win[0:size, :], kref[b], preferred_element_type=F32)
            for a in range(2):
                dest[a, start : start + size, b * LW : (b + 1) * LW] = res[
                    :, a * LW : (a + 1) * LW
                ].astype(BF16)

    def arrive(t, ch):
        start, size = send[ch]
        for slot in (0, 1, 4, 5):
            if ch == 0:
                wait_edge(t, slot)
            wait_row(t, slot, ch)
            lo = 0 if ch == 0 else PAD + start
            hi = PAD + start + size + (PAD if ch == len(send) - 1 else 0)
            widen(t, slot, lo, hi - lo)

    def transpose_row(slot, carry):
        for b in range(NB):
            row = pl.multiple_of(slot * LW, LW)
            xt[b, pl.ds(row, LW), 0:cols] = xs[b, slot, PAD : PAD + cols, :].T.astype(BF16)
            if kcols > cols:
                xt[b, pl.ds(row, LW), cols:kcols] = jnp.zeros((LW, kcols - cols), BF16)
        return carry

    lax.fori_loop(2, 4, transpose_row, 0)
    for ch in range(len(compute)):
        arrive(0, ch)
    lax.fori_loop(0, 2, transpose_row, 0)
    lax.fori_loop(4, 6, transpose_row, 0)

    wacc[...] = jnp.zeros(wacc.shape, F32)
    for b in range(NB):

        def weight_offset(m, carry):
            gbuf[...] = jnp.dot(xt[b], cw[b, m], preferred_element_type=F32)
            sums = [wacc[k * GW : (k + 1) * GW, b * LW : (b + 1) * LW] for k in range(K)]
            for a in range(2):
                for q in range(SMAX):
                    low = (a + q) * LW
                    part = gbuf[low : low + GW, a * LW : (a + 1) * LW]
                    for g in range(1, PB):
                        part = jnp.where(
                            group_of == g,
                            gbuf[low + g * GW : low + (g + 1) * GW, a * LW : (a + 1) * LW],
                            part,
                        )
                    for k in range(K):
                        sums[k] = sums[k] + tab[(a * SMAX + q) * (K * WIN) + k * WIN + m] * part
            for k in range(K):
                wacc[k * GW : (k + 1) * GW, b * LW : (b + 1) * LW] = sums[k]
            return carry

        lax.fori_loop(0, WIN, weight_offset, 0)
    for j in range(wacc.shape[0] // LW):
        turned = wacc[j * LW : (j + 1) * LW, :].T
        for to in range(lat_n):
            place = ((to // 8 + to) % 4) * n_shares + to // 4
            wt[place * share : (place + 1) * share, j * LW : (j + 1) * LW] = turned[
                to * share : (to + 1) * share
            ]

    half_rows, quarter_rows = C // 2, C // 4

    def half_copy():
        return pltpu.make_async_remote_copy(
            src_ref=wt.at[pl.ds(pl.multiple_of(sib * half_rows, 8), half_rows)],
            dst_ref=half,
            send_sem=sum_send.at[0],
            recv_sem=sum_recv.at[0],
            device_id=(lat, sib, ens),
            device_id_type=MESH,
        )

    def quarter_copy():
        low = pl.multiple_of(lon * half_rows + (1 - ens) * quarter_rows, 8)
        return pltpu.make_async_remote_copy(
            src_ref=wt.at[pl.ds(low, quarter_rows)],
            dst_ref=quarter,
            send_sem=sum_send.at[1],
            recv_sem=sum_recv.at[1],
            device_id=(lat, lon, 1 - ens),
            device_id_type=MESH,
        )

    def share_copy(j):
        to = share_lat(j)
        return to, pltpu.make_async_remote_copy(
            src_ref=wt.at[pl.ds(pl.multiple_of(mine * quarter_rows + j * share, 8), share)],
            dst_ref=shares.at[jnp.where(lat < to, lat, lat - 1)],
            send_sem=share_send.at[j],
            recv_sem=share_recv,
            device_id=(to, lon, ens),
            device_id_type=MESH,
        )

    def final_copy(j):
        return pltpu.make_async_remote_copy(
            src_ref=final,
            dst_ref=final,
            send_sem=final_send.at[j],
            recv_sem=final_recv,
            device_id=(lat, *partners[j]),
            device_id_type=MESH,
        )

    def sum_step(step):
        if step == 0:
            half_copy().start()
        elif step == 1:
            half_copy().wait()
            low = pl.multiple_of(lon * half_rows, 8)
            wt[pl.ds(low, half_rows), :] += half[...]
            quarter_copy().start()
        elif step == 2:
            quarter_copy().wait()
            low = pl.multiple_of(mine * quarter_rows, 8)
            wt[pl.ds(low, quarter_rows), :] += quarter[...]
            for j in range(n_shares):
                to, copy = share_copy(j)

                @pl.when(to != lat)
                def _():
                    copy.start()

        elif step == 3:

            @pl.when(owner)
            def _():
                pltpu.make_async_copy(shares, shares, share_recv).wait()
                low = pl.multiple_of(mine * quarter_rows + (lat // 4) * share, 8)

                def add(j, carry):
                    return carry + shares[j]

                total = lax.fori_loop(0, lat_n - 1, add, wt[pl.ds(low, share), :])
                final[...] = total * scale
                for j in range(3):
                    final_copy(j).start()

        else:

            @pl.when(jnp.logical_not(owner))
            def _():
                final_copy(0).wait_recv()

            for k in range(K):
                wout[k] = final[:, k * GW : (k + 1) * GW]

    sum_step(0)
    for ch in range(len(compute)):
        convolve(0, ch, kf, out, 1)
        if ch < 2:
            sum_step(ch + 1)
    for ch in range(len(compute)):
        arrive(1, ch)
        convolve(1, ch, ka, grad, -1)
        if ch == 0:
            sum_step(3)
    sum_step(4)

    for j in range(n_shares):
        to, copy = share_copy(j)

        @pl.when(to != lat)
        def _():
            copy.wait_send()

    @pl.when(owner)
    def _():
        for j in range(3):
            final_copy(j).wait_send()

    for t in range(2):
        edges_sent(t)
        for ch in range(len(send)):
            for dirn in range(2):
                for a in range(2):
                    row_copy(t, dirn, a, ch).wait_send()


def shards(fields, cotangent, weights, basis_values, support, counts):
    lat_n = lax.axis_size("lat")
    cols = fields.shape[2]
    share = C // lat_n
    wcols = -(-K * GW // LW) * LW
    total = 2 * lat_n * cols * lax.axis_size("lon") * lax.axis_size("ens") * fields.shape[0]
    kcols = -(-cols // 128) * 128
    n_chunks = len(chunks_of(cols)[0])
    w4 = weights.astype(F32).reshape(K, C // GW, GW, GW)
    wf = jnp.transpose(w4, (0, 3, 1, 2)).reshape(K, GW, C)
    wa = jnp.transpose(w4, (0, 2, 1, 3)).reshape(K, GW, C)
    vmem = pl.BlockSpec(memory_space=pltpu.VMEM)
    smem = pl.BlockSpec(memory_space=pltpu.SMEM)
    hbm = pl.BlockSpec(memory_space=pl.ANY)
    dma = pltpu.SemaphoreType.DMA
    out, grad, wgrad = pl.pallas_call(
        functools.partial(body, lat_n, cols, 1.0 / math.sqrt(total)),
        out_shape=(
            jax.ShapeDtypeStruct((2, cols, C), BF16),
            jax.ShapeDtypeStruct((2, cols, C), BF16),
            jax.ShapeDtypeStruct((K, share, GW), F32),
        ),
        in_specs=[hbm, hbm, vmem, vmem, smem, smem, smem],
        out_specs=(vmem, vmem, vmem),
        scratch_shapes=[
            pltpu.VMEM((PANEL, cols + 2 * PAD, C), BF16),
            pltpu.VMEM((PANEL, cols + 2 * PAD, C), BF16),
            pltpu.VMEM((NB, PANEL, cols + 2 * PAD, LW), F32),
            pltpu.VMEM((NB, PANEL, cols + 2 * PAD, LW), F32),
            pltpu.VMEM((NB, TAPS, 2 * LW), BF16),
            pltpu.VMEM((NB, TAPS, 2 * LW), BF16),
            pltpu.VMEM((NB, WIN, kcols, 2 * LW), BF16),
            pltpu.VMEM((NB, PANEL * LW, kcols), BF16),
            pltpu.VMEM((256, TAPS), BF16),
            pltpu.VMEM((PANEL * LW, 2 * LW), F32),
            pltpu.SMEM((2 * SMAX * K * WIN,), F32),
            pltpu.VMEM((wcols, C), F32),
            pltpu.VMEM((C, wcols), F32),
            pltpu.VMEM((C // 2, wcols), F32),
            pltpu.VMEM((C // 4, wcols), F32),
            pltpu.VMEM((lat_n - 1, share, wcols), F32),
            pltpu.VMEM((share, wcols), F32),
            dma((2, 2)),
            dma((2, 2, 2, n_chunks)),
            dma((2, PANEL, n_chunks)),
            dma((2, 3, 2, 2)),
            dma((2, PANEL, 2)),
            dma((2,)),
            dma((2,)),
            dma((lat_n // 4,)),
            dma,
            dma((3,)),
            dma,
        ],
        compiler_params=pltpu.CompilerParams(
            collective_id=0, has_side_effects=True, vmem_limit_bytes=56 * 1024 * 1024
        ),
        name="disco",
    )(
        fields[0],
        cotangent[0],
        wf,
        wa,
        basis_values.astype(F32).reshape(-1),
        support.reshape(-1),
        counts,
    )
    return (out[None], grad[None], wgrad)


def solution(mesh):
    placed = (P("ens", "lat", "lon", None), P("ens", "lat", "lon", None), P(), P(), P(), P())
    return jax.shard_map(
        shards,
        mesh=mesh,
        in_specs=placed,
        out_specs=(
            P("ens", "lat", "lon", None),
            P("ens", "lat", "lon", None),
            P(None, "lat", None),
        ),
        check_vma=False,
    )
```

```python
import functools
import math

import jax
import jax.numpy as jnp
from jax import lax
from jax.experimental import pallas as pl
from jax.experimental.pallas import tpu as pltpu
from jax.sharding import PartitionSpec as P

MESH = pl.DeviceIdType.MESH
BF16 = jnp.bfloat16
F32 = jnp.float32

C = 256
GW = 32
K = 9
SMAX = 5
WIN = 5
PAD = 16
LW = 128
NB = C // LW
PB = LW // GW
PANEL = 6
TAPS = PANEL * WIN * LW


def chunks_of(cols):
    starts = list(range(0, cols, 256))
    if len(starts) > 1 and cols - starts[-1] < 32:
        starts.pop()
    compute = [(s, (starts[j + 1] if j + 1 < len(starts) else cols) - s) for j, s in enumerate(starts)]
    cuts = [0] + [s + 16 for s in starts[1:]] + [cols]
    send = [(cuts[j], cuts[j + 1] - cuts[j]) for j in range(len(starts))]
    return compute, send


def body(
    lat_n,
    cols,
    scale,
    fields,
    cot,
    weights_hbm,
    basis_hbm,
    support_hbm,
    counts_hbm,
    out_hbm,
    grad_hbm,
    wout,
    xp,
    cp,
    xs,
    cs,
    kf,
    ka,
    cw,
    xt,
    out,
    grad,
    wf,
    wa,
    weights,
    basis_in,
    support,
    counts,
    basis_wide,
    basis,
    gbuf,
    tab,
    wacc,
    wt,
    half,
    quarter,
    shares,
    final,
    basis_sem,
    arg_sem,
    out_sem,
    own_sem,
    row_send,
    row_recv,
    edge_send,
    edge_recv,
    sum_send,
    sum_recv,
    share_send,
    share_recv,
    final_send,
    final_recv,
):
    compute, send = chunks_of(cols)
    kcols = cw.shape[2]
    lat = lax.axis_index("lat")
    lon = lax.axis_index("lon")
    ens = lax.axis_index("ens")
    sib = 1 - lon
    nlat = lat_n * 2
    top = lat == 0
    bottom = lat == lat_n - 1
    sources = (fields, cot)
    panels = (xp, cp)
    wides = (xs, cs)

    barrier = pltpu.get_barrier_semaphore()
    pl.semaphore_signal(barrier, inc=1, device_id=(lat, sib, ens), device_id_type=MESH)

    @pl.when(jnp.logical_not(top))
    def _():
        for to in (lon, sib):
            pl.semaphore_signal(barrier, inc=1, device_id=(lat - 1, to, ens), device_id_type=MESH)

    @pl.when(jnp.logical_not(bottom))
    def _():
        for to in (lon, sib):
            pl.semaphore_signal(barrier, inc=1, device_id=(lat + 1, to, ens), device_id_type=MESH)

    mine = lon * 2 + ens
    n_shares = lat_n // 4
    share = C // lat_n
    owner = lax.rem(lat // 8 + lat, 4) == mine
    partners = ((sib, ens), (lon, 1 - ens), (sib, 1 - ens))

    def share_lat(j):
        return 4 * j + lax.rem(mine - j // 2 + 4 * lat_n, 4)

    for to_lon, to_ens in partners[1:]:
        pl.semaphore_signal(barrier, inc=1, device_id=(lat, to_lon, to_ens), device_id_type=MESH)

    @pl.when(owner)
    def _():
        def greet(j, carry):
            pl.semaphore_signal(
                barrier, inc=1, device_id=(j + jnp.where(j < lat, 0, 1), lon, ens), device_id_type=MESH
            )
            return carry

        lax.fori_loop(0, lat_n - 1, greet, 0)

    pl.semaphore_wait(
        barrier,
        7
        + n_shares
        - jnp.where(owner, 1, 0)
        - 2 * jnp.where(top, 1, 0)
        - 2 * jnp.where(bottom, 1, 0),
    )

    def own_copy(t, a):
        return pltpu.make_async_copy(
            sources[t].at[a], panels[t].at[2 + a, pl.ds(PAD, cols)], own_sem.at[t, a]
        )

    def target(dirn, a):
        if dirn == 0:
            return (
                jnp.where(top, 0, lat - 1),
                jnp.where(top, sib, lon),
                jnp.where(top, 1 - a, 4 + a),
            )
        return (
            jnp.where(bottom, lat, lat + 1),
            jnp.where(bottom, sib, lon),
            jnp.where(bottom, 5 - a, a),
        )

    def row_copy(t, dirn, a, ch):
        to_lat, to_lon, slot = target(dirn, a)
        start, size = send[ch]
        return pltpu.make_async_remote_copy(
            src_ref=sources[t].at[a, pl.ds(start, size)],
            dst_ref=panels[t].at[slot, pl.ds(PAD + start, size)],
            send_sem=row_send.at[t, dirn, a, ch],
            recv_sem=row_recv.at[t, slot, ch],
            device_id=(to_lat, to_lon, ens),
            device_id_type=MESH,
        )

    def edge_refs(t, a, slot, side):
        src = sources[t].at[a, pl.ds(cols - PAD if side == 0 else 0, PAD)]
        dst = panels[t].at[slot, pl.ds(0 if side == 0 else PAD + cols, PAD)]
        return src, dst

    def edge_copy(t, where_to, a, slot, side, to_lat, to_lon):
        src, dst = edge_refs(t, a, slot, side)
        return pltpu.make_async_remote_copy(
            src_ref=src,
            dst_ref=dst,
            send_sem=edge_send.at[t, where_to, a, side],
            recv_sem=edge_recv.at[t, slot, side],
            device_id=(to_lat, to_lon, ens),
            device_id_type=MESH,
        )

    def edges(t):
        for a in range(2):
            for side in range(2):
                edge_copy(t, 2, a, 2 + a, side, lat, sib).start()
        for dirn, pole in ((0, top), (1, bottom)):
            for a in range(2):
                to_lat, _, slot = target(dirn, a)
                for side in range(2):

                    @pl.when(pole)
                    def _():
                        src, dst = edge_refs(t, a, slot, side)
                        pltpu.make_async_copy(src, dst, edge_recv.at[t, slot, side]).start()

                    @pl.when(jnp.logical_not(pole))
                    def _():
                        edge_copy(t, dirn, a, slot, side, to_lat, sib).start()

    def edges_sent(t):
        for a in range(2):
            for side in range(2):
                edge_copy(t, 2, a, 2 + a, side, lat, sib).wait_send()
        for dirn, pole in ((0, top), (1, bottom)):
            for a in range(2):
                to_lat, _, slot = target(dirn, a)
                for side in range(2):

                    @pl.when(jnp.logical_not(pole))
                    def _():
                        edge_copy(t, dirn, a, slot, side, to_lat, sib).wait_send()

    def wait_edge(t, slot):
        for side in range(2):
            src, dst = edge_refs(t, 0, slot, side)
            pltpu.make_async_copy(dst, dst, edge_recv.at[t, slot, side]).wait()

    def wait_row(t, slot, ch):
        start, size = send[ch]
        dst = panels[t].at[slot, pl.ds(PAD + start, size)]
        pltpu.make_async_copy(dst, dst, row_recv.at[t, slot, ch]).wait()

    def send_rows(t, ch, a):
        for dirn in range(2):
            row_copy(t, dirn, a, ch).start()

    n_chunks = len(send)
    for t in range(2):
        edges(t)
        for ch in range(n_chunks if t == 0 else 1):
            for a in range(2):
                send_rows(t, ch, a)
    small = [
        pltpu.make_async_copy(src, dst, arg_sem.at[j])
        for j, (src, dst) in enumerate(
            (
                (basis_hbm, basis_in),
                (support_hbm, support),
                (counts_hbm, counts),
                (weights_hbm, weights),
            )
        )
    ]
    for copy in small:
        copy.start()
    for t in range(2):
        for a in range(2):
            own_copy(t, a).start()
    later = [(ch, a) for ch in range(1, n_chunks) for a in range(2)]

    def send_later(count):
        for _ in range(min(count, len(later))):
            send_rows(1, *later.pop(0))

    small[0].wait()
    basis_wide[...] = basis_in[...].astype(F32)
    basis_copy = pltpu.make_async_copy(basis_wide, basis, basis_sem)
    basis_copy.start()
    for copy in small[1:]:
        copy.wait()
    for k in range(K):
        wide = weights[k].astype(F32)
        wf[k] = wide
        turned = wide.T
        wa[k] = jnp.concatenate([turned[g * GW : (g + 1) * GW] for g in range(C // GW)], axis=1)
    basis_copy.wait()

    group_of = lax.broadcasted_iota(jnp.int32, (GW, LW), 1) // GW

    def row_of(virtual):
        mirrored = jnp.logical_or(virtual < 0, virtual >= nlat)
        real = jnp.where(
            virtual < 0, -1 - virtual, jnp.where(virtual >= nlat, 2 * nlat - 1 - virtual, virtual)
        )
        return real, mirrored

    def coefficients(real, offset):
        first = support[0, real] - real
        slot = offset - first
        live = jnp.logical_and(slot >= 0, slot < counts[real])
        slot = jnp.minimum(jnp.maximum(slot, 0), SMAX - 1)
        gate = jnp.where(live, 1.0, 0.0).astype(F32)
        return [[basis[slot, k, m, real] * gate for m in range(WIN)] for k in range(K)]

    def spread(kref, wref, a, p, coef):
        for m0, m1 in ((0, 3), (3, 5)):
            sums = [jnp.zeros((GW, C), F32) for _ in range(m0, m1)]
            for k in range(K):
                wk = wref[k]
                for m in range(m0, m1):
                    sums[m - m0] = sums[m - m0] + coef[k][m] * wk
            for m in range(m0, m1):
                for b in range(NB):
                    part = sums[m - m0][:, b * LW : (b + 1) * LW]
                    for q in range(PB):
                        row = pl.multiple_of(p * (WIN * LW) + m * LW + q * GW, GW)
                        kref[b, pl.ds(row, GW), a * LW : (a + 1) * LW] = jnp.where(
                            group_of == q, part, 0.0
                        ).astype(BF16)

    for a in range(2):
        def forward_offset(q, carry):
            coef = coefficients(lat * 2 + a, q - 2)
            for k in range(K):
                for m in range(WIN):
                    tab[(a * SMAX + q) * (K * WIN) + k * WIN + m] = coef[k][m]
            spread(kf, wf, a, a + q, coef)
            return carry

        def adjoint_offset(q, carry):
            real, mirrored = row_of(lat * 2 - 2 + a + q)
            coef = coefficients(real, jnp.where(mirrored, q - 2, 2 - q))
            spread(ka, wa, a, a + q, coef)
            return carry

        lax.fori_loop(0, SMAX, forward_offset, 0)
        lax.fori_loop(0, SMAX, adjoint_offset, 0)
    for kref in (kf, ka):
        for b in range(NB):
            kref[b, 5 * WIN * LW :, 0:LW] = jnp.zeros((WIN * LW, LW), BF16)
            kref[b, 0 : WIN * LW, LW : 2 * LW] = jnp.zeros((WIN * LW, LW), BF16)

    def widen(t, slot, start, size):
        for b in range(NB):
            wides[t][b, slot, start : start + size, :] = panels[t][
                slot, start : start + size, b * LW : (b + 1) * LW
            ].astype(F32)

    for t in range(2):
        for a in range(2):
            own_copy(t, a).wait()
            wait_edge(t, 2 + a)
            widen(t, 2 + a, 0, cols + 2 * PAD)

    def own_windows(b, carry):
        for m in range(WIN):
            for a in range(2):
                cw[b, m, 0:cols, a * LW : (a + 1) * LW] = cs[
                    b, 2 + a, PAD + 2 - m : PAD + 2 - m + cols, :
                ].astype(BF16)
            if kcols > cols:
                cw[b, m, cols:kcols, :] = jnp.zeros((kcols - cols, 2 * LW), BF16)
        return carry

    lax.fori_loop(0, NB, own_windows, 0)

    def out_copy(t, ch):
        cells = pl.ds(compute[ch][0], compute[ch][1])
        return pltpu.make_async_copy(
            (out, grad)[t].at[:, cells], (out_hbm, grad_hbm)[t].at[:, cells], out_sem.at[t, ch]
        )

    def convolve(t, ch, kref, dest, sign):
        start, size = compute[ch]
        for b in range(NB):

            window = jnp.concatenate(
                [
                    wides[t][
                        b,
                        p,
                        PAD + start + sign * (m - 2) : PAD + start + sign * (m - 2) + size,
                        :,
                    ].astype(BF16)
                    for p in range(PANEL)
                    for m in range(WIN)
                ],
                axis=1,
            )
            res = jnp.dot(window, kref[b], preferred_element_type=F32)
            for a in range(2):
                dest[a, start : start + size, b * LW : (b + 1) * LW] = res[
                    :, a * LW : (a + 1) * LW
                ].astype(BF16)
        out_copy(t, ch).start()

    def arrive(t, ch):
        start, size = send[ch]
        for slot in (0, 1, 4, 5):
            if ch == 0:
                wait_edge(t, slot)
            wait_row(t, slot, ch)
            lo = 0 if ch == 0 else PAD + start
            hi = PAD + start + size + (PAD if ch == len(send) - 1 else 0)
            widen(t, slot, lo, hi - lo)

    def transpose_row(slot, carry):
        for b in range(NB):
            row = pl.multiple_of(jnp.where(slot < 2, slot + 2, jnp.where(slot < 4, slot - 2, slot)) * LW, LW)
            xt[b, pl.ds(row, LW), 0:cols] = xs[b, slot, PAD : PAD + cols, :].T.astype(BF16)
            if kcols > cols:
                xt[b, pl.ds(row, LW), cols:kcols] = jnp.zeros((LW, kcols - cols), BF16)
        return carry

    places = {2: 0, 3: 1, 0: 2, 1: 3, 4: 4, 5: 5}
    wacc[...] = jnp.zeros(wacc.shape, F32)

    def weight_gradient(lo, hi):
        for b in range(NB):

            def weight_offset(m, carry):
                gbuf[lo * LW : hi * LW, :] = jnp.dot(
                    xt[b, lo * LW : hi * LW, :], cw[b, m], preferred_element_type=F32
                )
                sums = [wacc[k * GW : (k + 1) * GW, b * LW : (b + 1) * LW] for k in range(K)]
                for a in range(2):
                    for q in range(SMAX):
                        if not lo <= places[a + q] < hi:
                            continue
                        low = places[a + q] * LW
                        part = gbuf[low : low + GW, a * LW : (a + 1) * LW]
                        for g in range(1, PB):
                            part = jnp.where(
                                group_of == g,
                                gbuf[low + g * GW : low + (g + 1) * GW, a * LW : (a + 1) * LW],
                                part,
                            )
                        for k in range(K):
                            sums[k] = (
                                sums[k] + tab[(a * SMAX + q) * (K * WIN) + k * WIN + m] * part
                            )
                for k in range(K):
                    wacc[k * GW : (k + 1) * GW, b * LW : (b + 1) * LW] = sums[k]
                return carry

            lax.fori_loop(0, WIN, weight_offset, 0)

    lax.fori_loop(2, 4, transpose_row, 0)
    weight_gradient(0, 2)
    last = len(compute) - 1
    for ch in range(last):
        arrive(0, ch)
        convolve(0, ch, kf, out, 1)
    arrive(0, last)
    lax.fori_loop(0, 2, transpose_row, 0)
    lax.fori_loop(4, 6, transpose_row, 0)
    weight_gradient(2, 6)
    for j in range(wacc.shape[0] // LW):
        turned = wacc[j * LW : (j + 1) * LW, :].T
        for to in range(lat_n):
            place = ((to // 8 + to) % 4) * n_shares + to // 4
            wt[place * share : (place + 1) * share, j * LW : (j + 1) * LW] = turned[
                to * share : (to + 1) * share
            ]

    half_rows, quarter_rows = C // 2, C // 4

    def half_copy():
        return pltpu.make_async_remote_copy(
            src_ref=wt.at[pl.ds(pl.multiple_of(sib * half_rows, 8), half_rows)],
            dst_ref=half,
            send_sem=sum_send.at[0],
            recv_sem=sum_recv.at[0],
            device_id=(lat, sib, ens),
            device_id_type=MESH,
        )

    def quarter_copy():
        low = pl.multiple_of(lon * half_rows + (1 - ens) * quarter_rows, 8)
        return pltpu.make_async_remote_copy(
            src_ref=wt.at[pl.ds(low, quarter_rows)],
            dst_ref=quarter,
            send_sem=sum_send.at[1],
            recv_sem=sum_recv.at[1],
            device_id=(lat, lon, 1 - ens),
            device_id_type=MESH,
        )

    def share_copy(j):
        to = share_lat(j)
        return to, pltpu.make_async_remote_copy(
            src_ref=wt.at[pl.ds(pl.multiple_of(mine * quarter_rows + j * share, 8), share)],
            dst_ref=shares.at[jnp.where(lat < to, lat, lat - 1)],
            send_sem=share_send.at[j],
            recv_sem=share_recv,
            device_id=(to, lon, ens),
            device_id_type=MESH,
        )

    def final_copy(j):
        return pltpu.make_async_remote_copy(
            src_ref=final,
            dst_ref=final,
            send_sem=final_send.at[j],
            recv_sem=final_recv,
            device_id=(lat, *partners[j]),
            device_id_type=MESH,
        )

    def sum_step(step):
        if step == 0:
            half_copy().start()
        elif step == 1:
            half_copy().wait()
            low = pl.multiple_of(lon * half_rows, 8)
            wt[pl.ds(low, half_rows), :] += half[...]
            quarter_copy().start()
        elif step == 2:
            quarter_copy().wait()
            low = pl.multiple_of(mine * quarter_rows, 8)
            wt[pl.ds(low, quarter_rows), :] += quarter[...]
            for j in range(n_shares):
                to, copy = share_copy(j)

                @pl.when(to != lat)
                def _():
                    copy.start()

        elif step == 3:

            @pl.when(owner)
            def _():
                pltpu.make_async_copy(shares, shares, share_recv).wait()
                low = pl.multiple_of(mine * quarter_rows + (lat // 4) * share, 8)

                def add(j, carry):
                    return carry + shares[j]

                total = lax.fori_loop(0, lat_n - 1, add, wt[pl.ds(low, share), :])
                final[...] = total * scale
                for j in range(3):
                    final_copy(j).start()

        else:

            @pl.when(jnp.logical_not(owner))
            def _():
                final_copy(0).wait_recv()

            for k in range(K):
                wout[k] = final[:, k * GW : (k + 1) * GW]

    sum_step(0)
    send_later(1)
    convolve(0, last, kf, out, 1)
    sum_step(1)
    send_later(1)
    for ch in range(len(compute)):
        if ch == last:
            send_later(len(later))
        arrive(1, ch)
        convolve(1, ch, ka, grad, -1)
        if ch == 0:
            sum_step(2)
            send_later(1)
        if ch == max(last - 1, 0):
            sum_step(3)
    sum_step(4)

    for j in range(n_shares):
        to, copy = share_copy(j)

        @pl.when(to != lat)
        def _():
            copy.wait_send()

    @pl.when(owner)
    def _():
        for j in range(3):
            final_copy(j).wait_send()

    for t in range(2):
        for ch in range(len(compute)):
            out_copy(t, ch).wait()
        edges_sent(t)
        for ch in range(len(send)):
            for dirn in range(2):
                for a in range(2):
                    row_copy(t, dirn, a, ch).wait_send()


def store(pieces, *refs):
    parts = []
    for j in range(3):
        src, dst, held = refs[j], refs[3 + j], refs[6 + j]
        size = src.shape[1] // pieces if j < 2 else src.shape[1]
        for n in range(pieces if j < 2 else 1):
            cells = (slice(None), pl.ds(n * size, size))
            parts.append(
                (
                    pltpu.make_async_copy(src.at[cells], held.at[cells], refs[9].at[j, n]),
                    pltpu.make_async_copy(held.at[cells], dst.at[cells], refs[10].at[j, n]),
                )
            )
    for bring, _ in parts:
        bring.start()
    for bring, take in parts:
        bring.wait()
        take.start()
    for _, take in parts:
        take.wait()


def shards(fields, cotangent, weights, basis_values, support, counts):
    lat_n = lax.axis_size("lat")
    cols = fields.shape[2]
    share = C // lat_n
    wcols = -(-K * GW // LW) * LW
    total = 2 * lat_n * cols * lax.axis_size("lon") * lax.axis_size("ens") * fields.shape[0]
    kcols = -(-cols // 128) * 128
    n_chunks = len(chunks_of(cols)[0])
    anywhere = pl.BlockSpec(memory_space=pl.ANY)
    dma = pltpu.SemaphoreType.DMA
    out, grad, wgrad = pl.pallas_call(
        functools.partial(body, lat_n, cols, 1.0 / math.sqrt(total)),
        out_shape=(
            jax.ShapeDtypeStruct((2, cols, C), BF16),
            jax.ShapeDtypeStruct((2, cols, C), BF16),
            jax.ShapeDtypeStruct((K, share, GW), F32),
        ),
        in_specs=[pl.BlockSpec(memory_space=pltpu.HBM)] * 6,
        out_specs=(anywhere, anywhere, pl.BlockSpec(memory_space=pltpu.VMEM)),
        scratch_shapes=[
            pltpu.VMEM((PANEL, cols + 2 * PAD, C), BF16),
            pltpu.VMEM((PANEL, cols + 2 * PAD, C), BF16),
            pltpu.VMEM((NB, PANEL, cols + 2 * PAD, LW), F32),
            pltpu.VMEM((NB, PANEL, cols + 2 * PAD, LW), F32),
            pltpu.VMEM((NB, TAPS, 2 * LW), BF16),
            pltpu.VMEM((NB, TAPS, 2 * LW), BF16),
            pltpu.VMEM((NB, WIN, kcols, 2 * LW), BF16),
            pltpu.VMEM((NB, PANEL * LW, kcols), BF16),
            pltpu.VMEM((2, cols, C), BF16),
            pltpu.VMEM((2, cols, C), BF16),
            pltpu.VMEM((K, GW, C), F32),
            pltpu.VMEM((K, GW, C), F32),
            pltpu.VMEM((K, GW, C), BF16),
            pltpu.VMEM((SMAX, K, WIN, 2 * lat_n), BF16),
            pltpu.SMEM((SMAX, 2 * lat_n), jnp.int32),
            pltpu.SMEM((2 * lat_n,), jnp.int32),
            pltpu.VMEM((SMAX, K, WIN, 2 * lat_n), F32),
            pltpu.SMEM((SMAX, K, WIN, 2 * lat_n), F32),
            pltpu.VMEM((PANEL * LW, 2 * LW), F32),
            pltpu.SMEM((2 * SMAX * K * WIN,), F32),
            pltpu.VMEM((wcols, C), F32),
            pltpu.VMEM((C, wcols), F32),
            pltpu.VMEM((C // 2, wcols), F32),
            pltpu.VMEM((C // 4, wcols), F32),
            pltpu.VMEM((lat_n - 1, share, wcols), F32),
            pltpu.VMEM((share, wcols), F32),
            dma,
            dma((4,)),
            dma((2, n_chunks)),
            dma((2, 2)),
            dma((2, 2, 2, n_chunks)),
            dma((2, PANEL, n_chunks)),
            dma((2, 3, 2, 2)),
            dma((2, PANEL, 2)),
            dma((2,)),
            dma((2,)),
            dma((lat_n // 4,)),
            dma,
            dma((3,)),
            dma,
        ],
        compiler_params=pltpu.CompilerParams(
            collective_id=0, has_side_effects=True, vmem_limit_bytes=61 * 1024 * 1024
        ),
        name="disco",
    )(
        fields[0],
        cotangent[0],
        jnp.transpose(weights, (0, 2, 1)),
        jnp.transpose(basis_values, (1, 2, 3, 0)),
        jnp.transpose(support),
        counts,
    )
    pieces = 3
    out, grad, wgrad = pl.pallas_call(
        functools.partial(store, pieces),
        out_shape=[jax.ShapeDtypeStruct(o.shape, o.dtype) for o in (out, grad, wgrad)],
        in_specs=[anywhere] * 3,
        out_specs=[anywhere] * 3,
        scratch_shapes=[
            pltpu.VMEM(out.shape, BF16),
            pltpu.VMEM(grad.shape, BF16),
            pltpu.VMEM(wgrad.shape, F32),
            dma((3, pieces)),
            dma((3, pieces)),
        ],
        compiler_params=pltpu.CompilerParams(vmem_limit_bytes=61 * 1024 * 1024),
        name="store",
    )(out, grad, wgrad)
    return (out[None], grad[None], wgrad)


def solution(mesh):
    placed = (P("ens", "lat", "lon", None), P("ens", "lat", "lon", None), P(), P(), P(), P())
    return jax.shard_map(
        shards,
        mesh=mesh,
        in_specs=placed,
        out_specs=(
            P("ens", "lat", "lon", None),
            P("ens", "lat", "lon", None),
            P(None, "lat", None),
        ),
        check_vma=False,
    )
```

```python
import functools
import math

import jax
import jax.numpy as jnp
from jax import lax
from jax.experimental import pallas as pl
from jax.experimental.pallas import tpu as pltpu
from jax.sharding import PartitionSpec as P

MESH = pl.DeviceIdType.MESH
BF16 = jnp.bfloat16
F32 = jnp.float32

C = 256
GW = 32
K = 9
SMAX = 5
WIN = 5
PAD = 16
LW = 128
NB = C // LW
PB = LW // GW
PANEL = 6
WIDTHS = (256, 304)
EARLY = 3
PACE = (1, 1, 1)
TAPS = PANEL * WIN * LW


def chunks_of(cols, width):
    starts = list(range(0, cols, width))
    if len(starts) > 1 and cols - starts[-1] < 32:
        starts.pop()
    compute = [(s, (starts[j + 1] if j + 1 < len(starts) else cols) - s) for j, s in enumerate(starts)]
    cuts = [0] + [s + 16 for s in starts[1:]] + [cols]
    send = [(cuts[j], cuts[j + 1] - cuts[j]) for j in range(len(starts))]
    pieces = []
    for start, size in send:
        first = -(-size // 32) * 16
        pieces.append([(start, first), (start + first, size - first)])
    return compute, pieces


def body(
    lat_n,
    cols,
    scale,
    fields,
    cot,
    weights_hbm,
    basis_hbm,
    support_hbm,
    counts_hbm,
    out_hbm,
    grad_hbm,
    wout,
    xp,
    cp,
    xs,
    cs,
    kf,
    ka,
    cw,
    xt,
    out,
    grad,
    wf,
    wa,
    weights,
    basis_in,
    support,
    counts,
    basis_wide,
    basis,
    gbuf,
    tab,
    wacc,
    wt,
    half,
    shares,
    final,
    basis_sem,
    arg_sem,
    out_sem,
    own_sem,
    row_send,
    row_recv,
    edge_send,
    edge_recv,
    sum_send,
    sum_recv,
    share_send,
    share_recv,
    final_send,
    final_recv,
):
    computes, sends = zip(*(chunks_of(cols, width) for width in WIDTHS))
    kcols = cw.shape[2]
    lat = lax.axis_index("lat")
    lon = lax.axis_index("lon")
    ens = lax.axis_index("ens")
    sib = 1 - lon
    nlat = lat_n * 2
    top = lat == 0
    bottom = lat == lat_n - 1
    sources = (fields, cot)
    panels = (xp, cp)
    wides = (xs, cs)

    barrier = pltpu.get_barrier_semaphore()
    pl.semaphore_signal(barrier, inc=1, device_id=(lat, sib, ens), device_id_type=MESH)

    @pl.when(jnp.logical_not(top))
    def _():
        for to in (lon, sib):
            pl.semaphore_signal(barrier, inc=1, device_id=(lat - 1, to, ens), device_id_type=MESH)

    @pl.when(jnp.logical_not(bottom))
    def _():
        for to in (lon, sib):
            pl.semaphore_signal(barrier, inc=1, device_id=(lat + 1, to, ens), device_id_type=MESH)

    n_shares = lat_n // 2
    share = C // lat_n
    owner = lax.rem(lat // 8 + lat, 2) == lon
    partners = ((sib, ens), (lon, 1 - ens), (sib, 1 - ens))

    def share_lat(j):
        return 2 * j + lax.rem(lon + j // 4, 2)

    for to_lon, to_ens in partners[1:]:
        pl.semaphore_signal(barrier, inc=1, device_id=(lat, to_lon, to_ens), device_id_type=MESH)

    @pl.when(owner)
    def _():
        def greet(j, carry):
            pl.semaphore_signal(
                barrier, inc=1, device_id=(j + jnp.where(j < lat, 0, 1), lon, ens), device_id_type=MESH
            )
            return carry

        lax.fori_loop(0, lat_n - 1, greet, 0)

    pl.semaphore_wait(
        barrier,
        7
        + n_shares
        - jnp.where(owner, 1, 0)
        - 2 * jnp.where(top, 1, 0)
        - 2 * jnp.where(bottom, 1, 0),
    )

    def own_copy(t, a):
        return pltpu.make_async_copy(
            sources[t].at[a], panels[t].at[2 + a, pl.ds(PAD, cols)], own_sem.at[t, a]
        )

    def target(dirn, a):
        if dirn == 0:
            return (
                jnp.where(top, 0, lat - 1),
                jnp.where(top, sib, lon),
                jnp.where(top, 1 - a, 4 + a),
            )
        return (
            jnp.where(bottom, lat, lat + 1),
            jnp.where(bottom, sib, lon),
            jnp.where(bottom, 5 - a, a),
        )

    def row_copy(t, dirn, a, ch, h):
        to_lat, to_lon, slot = target(dirn, a)
        start, size = sends[t][ch][h]
        return pltpu.make_async_remote_copy(
            src_ref=sources[t].at[a, pl.ds(start, size)],
            dst_ref=panels[t].at[slot, pl.ds(PAD + start, size)],
            send_sem=row_send.at[t, dirn, a, ch, h],
            recv_sem=row_recv.at[t, slot, ch, h],
            device_id=(to_lat, to_lon, ens),
            device_id_type=MESH,
        )

    def edge_refs(t, a, slot, side):
        src = sources[t].at[a, pl.ds(cols - PAD if side == 0 else 0, PAD)]
        dst = panels[t].at[slot, pl.ds(0 if side == 0 else PAD + cols, PAD)]
        return src, dst

    def edge_copy(t, where_to, a, slot, side, to_lat, to_lon):
        src, dst = edge_refs(t, a, slot, side)
        return pltpu.make_async_remote_copy(
            src_ref=src,
            dst_ref=dst,
            send_sem=edge_send.at[t, where_to, a, side],
            recv_sem=edge_recv.at[t, slot, side],
            device_id=(to_lat, to_lon, ens),
            device_id_type=MESH,
        )

    def edges(t):
        for a in range(2):
            for side in range(2):
                edge_copy(t, 2, a, 2 + a, side, lat, sib).start()
        for dirn, pole in ((0, top), (1, bottom)):
            for a in range(2):
                to_lat, _, slot = target(dirn, a)
                for side in range(2):

                    @pl.when(pole)
                    def _():
                        src, dst = edge_refs(t, a, slot, side)
                        pltpu.make_async_copy(src, dst, edge_recv.at[t, slot, side]).start()

                    @pl.when(jnp.logical_not(pole))
                    def _():
                        edge_copy(t, dirn, a, slot, side, to_lat, sib).start()

    def edges_sent(t):
        for a in range(2):
            for side in range(2):
                edge_copy(t, 2, a, 2 + a, side, lat, sib).wait_send()
        for dirn, pole in ((0, top), (1, bottom)):
            for a in range(2):
                to_lat, _, slot = target(dirn, a)
                for side in range(2):

                    @pl.when(jnp.logical_not(pole))
                    def _():
                        edge_copy(t, dirn, a, slot, side, to_lat, sib).wait_send()

    def wait_edge(t, slot):
        for side in range(2):
            src, dst = edge_refs(t, 0, slot, side)
            pltpu.make_async_copy(dst, dst, edge_recv.at[t, slot, side]).wait()

    def wait_row(t, slot, ch):
        for h in range(2):
            start, size = sends[t][ch][h]
            dst = panels[t].at[slot, pl.ds(PAD + start, size)]
            pltpu.make_async_copy(dst, dst, row_recv.at[t, slot, ch, h]).wait()

    def send_rows(t, ch, h):
        for a in range(2):
            for dirn in range(2):
                row_copy(t, dirn, a, ch, h).start()

    orders = [[(ch, h) for ch in range(len(send)) for h in range(2)] for send in sends]
    for t in range(2):
        edges(t)
        for ch, h in orders[0] if t == 0 else orders[1][:EARLY]:
            send_rows(t, ch, h)
    small = [
        pltpu.make_async_copy(src, dst, arg_sem.at[j])
        for j, (src, dst) in enumerate(
            (
                (basis_hbm, basis_in),
                (support_hbm, support),
                (counts_hbm, counts),
                (weights_hbm, weights),
            )
        )
    ]
    for copy in small:
        copy.start()
    for t in range(2):
        for a in range(2):
            own_copy(t, a).start()
    later = orders[1][EARLY:]

    def send_later(count):
        for _ in range(min(count, len(later))):
            send_rows(1, *later.pop(0))

    small[0].wait()
    basis_wide[...] = basis_in[...].astype(F32)
    basis_copy = pltpu.make_async_copy(basis_wide, basis, basis_sem)
    basis_copy.start()
    for copy in small[1:]:
        copy.wait()
    for k in range(K):
        wide = weights[k].astype(F32)
        wf[k] = wide
        turned = wide.T
        wa[k] = jnp.concatenate([turned[g * GW : (g + 1) * GW] for g in range(C // GW)], axis=1)
    basis_copy.wait()

    group_of = lax.broadcasted_iota(jnp.int32, (GW, LW), 1) // GW

    def row_of(virtual):
        mirrored = jnp.logical_or(virtual < 0, virtual >= nlat)
        real = jnp.where(
            virtual < 0, -1 - virtual, jnp.where(virtual >= nlat, 2 * nlat - 1 - virtual, virtual)
        )
        return real, mirrored

    def coefficients(real, offset):
        first = support[0, real] - real
        slot = offset - first
        live = jnp.logical_and(slot >= 0, slot < counts[real])
        slot = jnp.minimum(jnp.maximum(slot, 0), SMAX - 1)
        gate = jnp.where(live, 1.0, 0.0).astype(F32)
        return [[basis[slot, k, m, real] * gate for m in range(WIN)] for k in range(K)]

    def spread(kref, wref, a, p, coef):
        for m0, m1 in ((0, 3), (3, 5)):
            sums = [jnp.zeros((GW, C), F32) for _ in range(m0, m1)]
            for k in range(K):
                wk = wref[k]
                for m in range(m0, m1):
                    sums[m - m0] = sums[m - m0] + coef[k][m] * wk
            for m in range(m0, m1):
                for b in range(NB):
                    part = sums[m - m0][:, b * LW : (b + 1) * LW]
                    for q in range(PB):
                        row = pl.multiple_of(p * (WIN * LW) + m * LW + q * GW, GW)
                        kref[b, pl.ds(row, GW), a * LW : (a + 1) * LW] = jnp.where(
                            group_of == q, part, 0.0
                        ).astype(BF16)

    for a in range(2):
        def forward_offset(q, carry):
            coef = coefficients(lat * 2 + a, q - 2)
            for k in range(K):
                for m in range(WIN):
                    tab[(a * SMAX + q) * (K * WIN) + k * WIN + m] = coef[k][m]
            spread(kf, wf, a, a + q, coef)
            return carry

        def adjoint_offset(q, carry):
            real, mirrored = row_of(lat * 2 - 2 + a + q)
            coef = coefficients(real, jnp.where(mirrored, q - 2, 2 - q))
            spread(ka, wa, a, a + q, coef)
            return carry

        lax.fori_loop(0, SMAX, forward_offset, 0)
        lax.fori_loop(0, SMAX, adjoint_offset, 0)
    for kref in (kf, ka):
        for b in range(NB):
            kref[b, 5 * WIN * LW :, 0:LW] = jnp.zeros((WIN * LW, LW), BF16)
            kref[b, 0 : WIN * LW, LW : 2 * LW] = jnp.zeros((WIN * LW, LW), BF16)

    def widen(t, slot, start, size):
        for b in range(NB):
            wides[t][b, slot, start : start + size, :] = panels[t][
                slot, start : start + size, b * LW : (b + 1) * LW
            ].astype(F32)

    for t in range(2):
        for a in range(2):
            own_copy(t, a).wait()
            wait_edge(t, 2 + a)
            widen(t, 2 + a, 0, cols + 2 * PAD)

    def own_windows(b, carry):
        for m in range(WIN):
            for a in range(2):
                cw[b, m, 0:cols, a * LW : (a + 1) * LW] = cs[
                    b, 2 + a, PAD + 2 - m : PAD + 2 - m + cols, :
                ].astype(BF16)
            if kcols > cols:
                cw[b, m, cols:kcols, :] = jnp.zeros((kcols - cols, 2 * LW), BF16)
        return carry

    lax.fori_loop(0, NB, own_windows, 0)

    def out_copy(t, ch):
        cells = pl.ds(*computes[t][ch])
        return pltpu.make_async_copy(
            (out, grad)[t].at[:, cells], (out_hbm, grad_hbm)[t].at[:, cells], out_sem.at[t, ch]
        )

    def convolve(t, ch, kref, dest, sign):
        start, size = computes[t][ch]
        for b in range(NB):

            window = jnp.concatenate(
                [
                    wides[t][
                        b,
                        p,
                        PAD + start + sign * (m - 2) : PAD + start + sign * (m - 2) + size,
                        :,
                    ].astype(BF16)
                    for p in range(PANEL)
                    for m in range(WIN)
                ],
                axis=1,
            )
            res = jnp.dot(window, kref[b], preferred_element_type=F32)
            for a in range(2):
                dest[a, start : start + size, b * LW : (b + 1) * LW] = res[
                    :, a * LW : (a + 1) * LW
                ].astype(BF16)
        out_copy(t, ch).start()

    def arrive(t, ch):
        send = sends[t]
        start, size = send[ch][0][0], send[ch][0][1] + send[ch][1][1]
        for slot in (0, 1, 4, 5):
            if ch == 0:
                wait_edge(t, slot)
            wait_row(t, slot, ch)
            lo = 0 if ch == 0 else PAD + start
            hi = PAD + start + size + (PAD if ch == len(send) - 1 else 0)
            widen(t, slot, lo, hi - lo)

    def transpose_rows(slots, start, end):
        def transpose_row(slot, carry):
            for b in range(NB):
                place = jnp.where(slot < 2, slot + 2, jnp.where(slot < 4, slot - 2, slot))
                row = pl.multiple_of(place * LW, LW)
                xt[b, pl.ds(row, LW), start:end] = xs[
                    b, slot, PAD + start : PAD + end, :
                ].T.astype(BF16)
                if end == cols and kcols > cols:
                    xt[b, pl.ds(row, LW), cols:kcols] = jnp.zeros((LW, kcols - cols), BF16)
            return carry

        lax.fori_loop(*slots, transpose_row, 0)

    places = {2: 0, 3: 1, 0: 2, 1: 3, 4: 4, 5: 5}
    wacc[...] = jnp.zeros(wacc.shape, F32)

    def weight_gradient(lo, hi, start, end):
        for b in range(NB):

            def weight_offset(m, carry):
                gbuf[lo * LW : hi * LW, :] = jnp.dot(
                    xt[b, lo * LW : hi * LW, start:end],
                    cw[b, m, start:end],
                    preferred_element_type=F32
                )
                sums = [wacc[k * GW : (k + 1) * GW, b * LW : (b + 1) * LW] for k in range(K)]
                for a in range(2):
                    for q in range(SMAX):
                        if not lo <= places[a + q] < hi:
                            continue
                        low = places[a + q] * LW
                        part = gbuf[low : low + GW, a * LW : (a + 1) * LW]
                        for g in range(1, PB):
                            part = jnp.where(
                                group_of == g,
                                gbuf[low + g * GW : low + (g + 1) * GW, a * LW : (a + 1) * LW],
                                part,
                            )
                        for k in range(K):
                            sums[k] = (
                                sums[k] + tab[(a * SMAX + q) * (K * WIN) + k * WIN + m] * part
                            )
                for k in range(K):
                    wacc[k * GW : (k + 1) * GW, b * LW : (b + 1) * LW] = sums[k]
                return carry

            lax.fori_loop(0, WIN, weight_offset, 0)

    transpose_rows((2, 4), 0, cols)
    weight_gradient(0, 2, 0, kcols)
    compute = computes[0]
    last = len(compute) - 1
    for ch in range(len(compute)):
        arrive(0, ch)
        start, end = compute[ch][0], compute[ch][0] + compute[ch][1]
        for slots in ((0, 2), (4, 6)):
            transpose_rows(slots, start, end)
        weight_gradient(2, 6, start, kcols if ch == last else end)
        if ch < last:
            convolve(0, ch, kf, out, 1)
    for j in range(wacc.shape[0] // LW):
        turned = wacc[j * LW : (j + 1) * LW, :].T
        for to in range(lat_n):
            place = ((to // 8 + to) % 2) * n_shares + to // 2
            wt[place * share : (place + 1) * share, j * LW : (j + 1) * LW] = turned[
                to * share : (to + 1) * share
            ]

    half_rows = C // 2

    def half_copy():
        return pltpu.make_async_remote_copy(
            src_ref=wt.at[pl.ds(pl.multiple_of(sib * half_rows, 8), half_rows)],
            dst_ref=half,
            send_sem=sum_send.at[0],
            recv_sem=sum_recv.at[0],
            device_id=(lat, sib, ens),
            device_id_type=MESH,
        )

    def share_copy(j):
        to = share_lat(j)
        return to, pltpu.make_async_remote_copy(
            src_ref=wt.at[pl.ds(pl.multiple_of(lon * half_rows + j * share, 8), share)],
            dst_ref=shares.at[jnp.where(lat < to, lat, lat - 1)],
            send_sem=share_send.at[j],
            recv_sem=share_recv,
            device_id=(to, lon, ens),
            device_id_type=MESH,
        )

    def final_copy(j):
        return pltpu.make_async_remote_copy(
            src_ref=final.at[ens],
            dst_ref=final.at[ens],
            send_sem=final_send.at[j],
            recv_sem=final_recv.at[ens],
            device_id=(lat, *partners[j]),
            device_id_type=MESH,
        )

    def sum_step(step):
        if step == 0:
            half_copy().start()
        elif step == 1:
            half_copy().wait()
            low = pl.multiple_of(lon * half_rows, 8)
            wt[pl.ds(low, half_rows), :] += half[...]
            for j in range(n_shares):
                to, copy = share_copy(j)

                @pl.when(to != lat)
                def _():
                    copy.start()

        elif step == 2:

            @pl.when(owner)
            def _():
                pltpu.make_async_copy(shares, shares, share_recv).wait()
                low = pl.multiple_of(lon * half_rows + (lat // 2) * share, 8)

                def add(j, carry):
                    return carry + shares[j]

                final[ens] = lax.fori_loop(0, lat_n - 1, add, wt[pl.ds(low, share), :])
                for j in range(3):
                    final_copy(j).start()

        else:
            for e in range(2):

                @pl.when(jnp.logical_not(jnp.logical_and(owner, ens == e)))
                def _():
                    part = final.at[e]
                    pltpu.make_async_copy(part, part, final_recv.at[e]).wait()

            total = (final[0] + final[1]) * scale
            for k in range(K):
                wout[k] = total[:, k * GW : (k + 1) * GW]

    sum_step(0)
    send_later(PACE[0])
    convolve(0, last, kf, out, 1)
    sum_step(1)
    send_later(PACE[1])
    last = len(computes[1]) - 1
    for ch in range(last + 1):
        send_later(len([c for c, _ in later if c <= ch]))
        arrive(1, ch)
        convolve(1, ch, ka, grad, -1)
        if ch == 0:
            send_later(PACE[2])
        if ch == max(last - 1, 0):
            sum_step(2)
    sum_step(3)

    for j in range(n_shares):
        to, copy = share_copy(j)

        @pl.when(to != lat)
        def _():
            copy.wait_send()

    @pl.when(owner)
    def _():
        for j in range(3):
            final_copy(j).wait_send()

    for t in range(2):
        for ch in range(len(computes[t])):
            out_copy(t, ch).wait()
        edges_sent(t)
        for ch in range(len(sends[t])):
            for dirn in range(2):
                for a in range(2):
                    for h in range(2):
                        row_copy(t, dirn, a, ch, h).wait_send()


def store(pieces, *refs):
    parts = []
    for j in range(3):
        src, dst, held = refs[j], refs[3 + j], refs[6 + j]
        size = src.shape[1] // pieces if j < 2 else src.shape[1]
        for n in range(pieces if j < 2 else 1):
            cells = (slice(None), pl.ds(n * size, size))
            parts.append(
                (
                    pltpu.make_async_copy(src.at[cells], held.at[cells], refs[9].at[j, n]),
                    pltpu.make_async_copy(held.at[cells], dst.at[cells], refs[10].at[j, n]),
                )
            )
    for bring, _ in parts:
        bring.start()
    for bring, take in parts:
        bring.wait()
        take.start()
    for _, take in parts:
        take.wait()


def shards(fields, cotangent, weights, basis_values, support, counts):
    lat_n = lax.axis_size("lat")
    cols = fields.shape[2]
    share = C // lat_n
    wcols = -(-K * GW // LW) * LW
    total = 2 * lat_n * cols * lax.axis_size("lon") * lax.axis_size("ens") * fields.shape[0]
    kcols = -(-cols // 128) * 128
    n_chunks = max(len(chunks_of(cols, width)[0]) for width in WIDTHS)
    anywhere = pl.BlockSpec(memory_space=pl.ANY)
    dma = pltpu.SemaphoreType.DMA
    out, grad, wgrad = pl.pallas_call(
        functools.partial(body, lat_n, cols, 1.0 / math.sqrt(total)),
        out_shape=(
            jax.ShapeDtypeStruct((2, cols, C), BF16),
            jax.ShapeDtypeStruct((2, cols, C), BF16),
            jax.ShapeDtypeStruct((K, share, GW), F32),
        ),
        in_specs=[pl.BlockSpec(memory_space=pltpu.HBM)] * 6,
        out_specs=(anywhere, anywhere, pl.BlockSpec(memory_space=pltpu.VMEM)),
        scratch_shapes=[
            pltpu.VMEM((PANEL, cols + 2 * PAD, C), BF16),
            pltpu.VMEM((PANEL, cols + 2 * PAD, C), BF16),
            pltpu.VMEM((NB, PANEL, cols + 2 * PAD, LW), F32),
            pltpu.VMEM((NB, PANEL, cols + 2 * PAD, LW), F32),
            pltpu.VMEM((NB, TAPS, 2 * LW), BF16),
            pltpu.VMEM((NB, TAPS, 2 * LW), BF16),
            pltpu.VMEM((NB, WIN, kcols, 2 * LW), BF16),
            pltpu.VMEM((NB, PANEL * LW, kcols), BF16),
            pltpu.VMEM((2, cols, C), BF16),
            pltpu.VMEM((2, cols, C), BF16),
            pltpu.VMEM((K, GW, C), F32),
            pltpu.VMEM((K, GW, C), F32),
            pltpu.VMEM((K, GW, C), BF16),
            pltpu.VMEM((SMAX, K, WIN, 2 * lat_n), BF16),
            pltpu.SMEM((SMAX, 2 * lat_n), jnp.int32),
            pltpu.SMEM((2 * lat_n,), jnp.int32),
            pltpu.VMEM((SMAX, K, WIN, 2 * lat_n), F32),
            pltpu.SMEM((SMAX, K, WIN, 2 * lat_n), F32),
            pltpu.VMEM((PANEL * LW, 2 * LW), F32),
            pltpu.SMEM((2 * SMAX * K * WIN,), F32),
            pltpu.VMEM((wcols, C), F32),
            pltpu.VMEM((C, wcols), F32),
            pltpu.VMEM((C // 2, wcols), F32),
            pltpu.VMEM((lat_n - 1, share, wcols), F32),
            pltpu.VMEM((2, share, wcols), F32),
            dma,
            dma((4,)),
            dma((2, n_chunks)),
            dma((2, 2)),
            dma((2, 2, 2, n_chunks, 2)),
            dma((2, PANEL, n_chunks, 2)),
            dma((2, 3, 2, 2)),
            dma((2, PANEL, 2)),
            dma((1,)),
            dma((1,)),
            dma((lat_n // 2,)),
            dma,
            dma((3,)),
            dma((2,)),
        ],
        compiler_params=pltpu.CompilerParams(
            collective_id=0, has_side_effects=True, vmem_limit_bytes=61 * 1024 * 1024
        ),
        name="disco",
    )(
        fields[0],
        cotangent[0],
        jnp.transpose(weights, (0, 2, 1)),
        jnp.transpose(basis_values, (1, 2, 3, 0)),
        jnp.transpose(support),
        counts,
    )
    pieces = 3
    out, grad, wgrad = pl.pallas_call(
        functools.partial(store, pieces),
        out_shape=[jax.ShapeDtypeStruct(o.shape, o.dtype) for o in (out, grad, wgrad)],
        in_specs=[anywhere] * 3,
        out_specs=[anywhere] * 3,
        scratch_shapes=[
            pltpu.VMEM(out.shape, BF16),
            pltpu.VMEM(grad.shape, BF16),
            pltpu.VMEM(wgrad.shape, F32),
            dma((3, pieces)),
            dma((3, pieces)),
        ],
        compiler_params=pltpu.CompilerParams(vmem_limit_bytes=61 * 1024 * 1024),
        name="store",
    )(out, grad, wgrad)
    return (out[None], grad[None], wgrad)


def solution(mesh):
    placed = (P("ens", "lat", "lon", None), P("ens", "lat", "lon", None), P(), P(), P(), P())
    return jax.shard_map(
        shards,
        mesh=mesh,
        in_specs=placed,
        out_specs=(
            P("ens", "lat", "lon", None),
            P("ens", "lat", "lon", None),
            P(None, "lat", None),
        ),
        check_vma=False,
    )
```

```python
import functools
import math

import jax
import jax.numpy as jnp
from jax import lax
from jax.experimental import pallas as pl
from jax.experimental.pallas import tpu as pltpu
from jax.sharding import PartitionSpec as P

MESH = pl.DeviceIdType.MESH
BF16 = jnp.bfloat16
F32 = jnp.float32

C = 256
GW = 32
K = 9
SMAX = 5
WIN = 5
PAD = 16
LW = 128
NB = C // LW
PB = LW // GW
PANEL = 6
HALO = (0, 1, 4, 5)
WIDTHS = (256, 304)
EARLY = 3
PACE = (1, 1, 1)
TAPS = PANEL * WIN * LW


def chunks_of(cols, width):
    starts = list(range(0, cols, width))
    if len(starts) > 1 and cols - starts[-1] < 32:
        starts.pop()
    compute = [(s, (starts[j + 1] if j + 1 < len(starts) else cols) - s) for j, s in enumerate(starts)]
    cuts = [0] + [s + PAD for s in starts[1:]] + [cols - PAD]
    send = [(cuts[j], cuts[j + 1] - cuts[j]) for j in range(len(starts))]
    pieces = []
    for start, size in send:
        first = -(-size // 32) * 16
        pieces.append([(start, first), (start + first, size - first)])
    return compute, pieces


def body(
    lat_n,
    cols,
    scale,
    fields,
    cot,
    weights_hbm,
    basis_hbm,
    support_hbm,
    counts_hbm,
    out_hbm,
    grad_hbm,
    wout,
    xp,
    cp,
    xs,
    cs,
    kf,
    ka,
    cw,
    xt,
    out,
    grad,
    wf,
    wa,
    weights,
    basis_in,
    support,
    counts,
    basis_wide,
    basis,
    gbuf,
    tab,
    wacc,
    wt,
    half,
    shares,
    final,
    basis_sem,
    arg_sem,
    out_sem,
    own_sem,
    row_send,
    row_recv,
    edge_send,
    edge_recv,
    last_send,
    last_recv,
    sum_send,
    sum_recv,
    share_send,
    share_recv,
    final_send,
    final_recv,
):
    computes, sends = zip(*(chunks_of(cols, width) for width in WIDTHS))
    kcols = cw.shape[2]
    lat = lax.axis_index("lat")
    lon = lax.axis_index("lon")
    ens = lax.axis_index("ens")
    sib = 1 - lon
    nlat = lat_n * 2
    top = lat == 0
    bottom = lat == lat_n - 1
    sources = (fields, cot)
    panels = (xp, cp)
    wides = (xs, cs)

    barrier = pltpu.get_barrier_semaphore()
    pl.semaphore_signal(barrier, inc=1, device_id=(lat, sib, ens), device_id_type=MESH)

    @pl.when(jnp.logical_not(top))
    def _():
        pl.semaphore_signal(barrier, inc=1, device_id=(lat - 1, lon, ens), device_id_type=MESH)

    @pl.when(jnp.logical_not(bottom))
    def _():
        pl.semaphore_signal(barrier, inc=1, device_id=(lat + 1, lon, ens), device_id_type=MESH)

    n_shares = lat_n // 2
    share = C // lat_n
    owner = lax.rem(lat // 8 + lat, 2) == lon
    partners = ((sib, ens), (lon, 1 - ens), (sib, 1 - ens))

    def share_lat(j):
        return 2 * j + lax.rem(lon + j // 4, 2)

    for to_lon, to_ens in partners[1:]:
        pl.semaphore_signal(barrier, inc=1, device_id=(lat, to_lon, to_ens), device_id_type=MESH)

    @pl.when(owner)
    def _():
        def greet(j, carry):
            pl.semaphore_signal(
                barrier, inc=1, device_id=(j + jnp.where(j < lat, 0, 1), lon, ens), device_id_type=MESH
            )
            return carry

        lax.fori_loop(0, lat_n - 1, greet, 0)

    pl.semaphore_wait(
        barrier,
        5
        + n_shares
        - jnp.where(owner, 1, 0)
        - jnp.where(top, 1, 0)
        - jnp.where(bottom, 1, 0),
    )

    def own_copy(t, a):
        return pltpu.make_async_copy(
            sources[t].at[a], panels[t].at[2 + a, pl.ds(PAD, cols)], own_sem.at[t, a]
        )

    def target(dirn, a):
        if dirn == 0:
            return (
                jnp.where(top, 0, lat - 1),
                jnp.where(top, sib, lon),
                jnp.where(top, 1 - a, 4 + a),
            )
        return (
            jnp.where(bottom, lat, lat + 1),
            jnp.where(bottom, sib, lon),
            jnp.where(bottom, 5 - a, a),
        )

    def row_copy(t, dirn, a, ch, h):
        to_lat, to_lon, slot = target(dirn, a)
        start, size = sends[t][ch][h]
        return pltpu.make_async_remote_copy(
            src_ref=sources[t].at[a, pl.ds(start, size)],
            dst_ref=panels[t].at[slot, pl.ds(PAD + start, size)],
            send_sem=row_send.at[t, dirn, a, ch, h],
            recv_sem=row_recv.at[t, slot, ch, h],
            device_id=(to_lat, to_lon, ens),
            device_id_type=MESH,
        )

    def edge_copy(t, slot, side):
        cells = pl.ds(cols - PAD if side == 0 else 0, PAD)
        if slot in (2, 3):
            src = sources[t].at[slot - 2, cells]
        else:
            src = panels[t].at[slot, pl.ds(cols if side == 0 else PAD, PAD)]
        return pltpu.make_async_remote_copy(
            src_ref=src,
            dst_ref=panels[t].at[slot, pl.ds(0 if side == 0 else PAD + cols, PAD)],
            send_sem=edge_send.at[t, slot, side],
            recv_sem=edge_recv.at[t, slot, side],
            device_id=(lat, sib, ens),
            device_id_type=MESH,
        )

    def wait_edge(t, slot, side):
        edge_copy(t, slot, side).wait_recv()

    def last_copy(t, dirn, a):
        to_lat, to_lon, slot = target(dirn, a)
        return pltpu.make_async_remote_copy(
            src_ref=sources[t].at[a, pl.ds(cols - PAD, PAD)],
            dst_ref=panels[t].at[slot, pl.ds(cols, PAD)],
            send_sem=last_send.at[t, dirn, a],
            recv_sem=last_recv.at[t, slot],
            device_id=(to_lat, to_lon, ens),
            device_id_type=MESH,
        )

    def forward_last(t):
        for slot in HALO:
            dst = panels[t].at[slot, pl.ds(cols, PAD)]
            pltpu.make_async_copy(dst, dst, last_recv.at[t, slot]).wait()
            edge_copy(t, slot, 0).start()

    def wait_row(t, slot, ch):
        for h in range(2):
            start, size = sends[t][ch][h]
            dst = panels[t].at[slot, pl.ds(PAD + start, size)]
            pltpu.make_async_copy(dst, dst, row_recv.at[t, slot, ch, h]).wait()

    def send_rows(t, ch, h):
        for a in range(2):
            for dirn in range(2):
                row_copy(t, dirn, a, ch, h).start()

    orders = [[(ch, h) for ch in range(len(send)) for h in range(2)] for send in sends]
    for t in range(2):
        for a in range(2):
            for side in range(2):
                edge_copy(t, 2 + a, side).start()
            for dirn in range(2):
                last_copy(t, dirn, a).start()
        for ch, h in orders[0] if t == 0 else orders[1][:EARLY]:
            send_rows(t, ch, h)
    small = [
        pltpu.make_async_copy(src, dst, arg_sem.at[j])
        for j, (src, dst) in enumerate(
            (
                (basis_hbm, basis_in),
                (support_hbm, support),
                (counts_hbm, counts),
                (weights_hbm, weights),
            )
        )
    ]
    for copy in small:
        copy.start()
    for t in range(2):
        for a in range(2):
            own_copy(t, a).start()
    later = orders[1][EARLY:]

    def send_later(count):
        for _ in range(min(count, len(later))):
            send_rows(1, *later.pop(0))

    small[0].wait()
    basis_wide[...] = basis_in[...].astype(F32)
    basis_copy = pltpu.make_async_copy(basis_wide, basis, basis_sem)
    basis_copy.start()
    for copy in small[1:]:
        copy.wait()
    for k in range(K):
        wide = weights[k].astype(F32)
        wf[k] = wide
        turned = wide.T
        wa[k] = jnp.concatenate([turned[g * GW : (g + 1) * GW] for g in range(C // GW)], axis=1)
    basis_copy.wait()

    group_of = lax.broadcasted_iota(jnp.int32, (GW, LW), 1) // GW

    def row_of(virtual):
        mirrored = jnp.logical_or(virtual < 0, virtual >= nlat)
        real = jnp.where(
            virtual < 0, -1 - virtual, jnp.where(virtual >= nlat, 2 * nlat - 1 - virtual, virtual)
        )
        return real, mirrored

    def coefficients(real, offset):
        first = support[0, real] - real
        slot = offset - first
        live = jnp.logical_and(slot >= 0, slot < counts[real])
        slot = jnp.minimum(jnp.maximum(slot, 0), SMAX - 1)
        gate = jnp.where(live, 1.0, 0.0).astype(F32)
        return [[basis[slot, k, m, real] * gate for m in range(WIN)] for k in range(K)]

    def spread(kref, wref, a, p, coef):
        for m0, m1 in ((0, 3), (3, 5)):
            sums = [jnp.zeros((GW, C), F32) for _ in range(m0, m1)]
            for k in range(K):
                wk = wref[k]
                for m in range(m0, m1):
                    sums[m - m0] = sums[m - m0] + coef[k][m] * wk
            for m in range(m0, m1):
                for b in range(NB):
                    part = sums[m - m0][:, b * LW : (b + 1) * LW]
                    for q in range(PB):
                        row = pl.multiple_of(p * (WIN * LW) + m * LW + q * GW, GW)
                        kref[b, pl.ds(row, GW), a * LW : (a + 1) * LW] = jnp.where(
                            group_of == q, part, 0.0
                        ).astype(BF16)

    for a in range(2):
        def forward_offset(q, carry):
            coef = coefficients(lat * 2 + a, q - 2)
            for k in range(K):
                for m in range(WIN):
                    tab[(a * SMAX + q) * (K * WIN) + k * WIN + m] = coef[k][m]
            spread(kf, wf, a, a + q, coef)
            return carry

        def adjoint_offset(q, carry):
            real, mirrored = row_of(lat * 2 - 2 + a + q)
            coef = coefficients(real, jnp.where(mirrored, q - 2, 2 - q))
            spread(ka, wa, a, a + q, coef)
            return carry

        lax.fori_loop(0, SMAX, forward_offset, 0)
        lax.fori_loop(0, SMAX, adjoint_offset, 0)
    for kref in (kf, ka):
        for b in range(NB):
            kref[b, 5 * WIN * LW :, 0:LW] = jnp.zeros((WIN * LW, LW), BF16)
            kref[b, 0 : WIN * LW, LW : 2 * LW] = jnp.zeros((WIN * LW, LW), BF16)

    def widen(t, slot, start, size):
        for b in range(NB):
            wides[t][b, slot, start : start + size, :] = panels[t][
                slot, start : start + size, b * LW : (b + 1) * LW
            ].astype(F32)

    for t in range(2):
        for a in range(2):
            own_copy(t, a).wait()
            for side in range(2):
                wait_edge(t, 2 + a, side)
            widen(t, 2 + a, 0, cols + 2 * PAD)

    def own_windows(b, carry):
        for m in range(WIN):
            for a in range(2):
                cw[b, m, 0:cols, a * LW : (a + 1) * LW] = cs[
                    b, 2 + a, PAD + 2 - m : PAD + 2 - m + cols, :
                ].astype(BF16)
            if kcols > cols:
                cw[b, m, cols:kcols, :] = jnp.zeros((kcols - cols, 2 * LW), BF16)
        return carry

    lax.fori_loop(0, NB, own_windows, 0)

    def out_copy(t, ch):
        cells = pl.ds(*computes[t][ch])
        return pltpu.make_async_copy(
            (out, grad)[t].at[:, cells], (out_hbm, grad_hbm)[t].at[:, cells], out_sem.at[t, ch]
        )

    def convolve(t, ch, kref, dest, sign):
        start, size = computes[t][ch]
        for b in range(NB):

            window = jnp.concatenate(
                [
                    wides[t][
                        b,
                        p,
                        PAD + start + sign * (m - 2) : PAD + start + sign * (m - 2) + size,
                        :,
                    ].astype(BF16)
                    for p in range(PANEL)
                    for m in range(WIN)
                ],
                axis=1,
            )
            res = jnp.dot(window, kref[b], preferred_element_type=F32)
            for a in range(2):
                dest[a, start : start + size, b * LW : (b + 1) * LW] = res[
                    :, a * LW : (a + 1) * LW
                ].astype(BF16)
        out_copy(t, ch).start()

    def arrive(t, ch):
        send = sends[t]
        start, size = send[ch][0][0], send[ch][0][1] + send[ch][1][1]
        if ch == 0:
            forward_last(t)
        for slot in HALO:
            wait_row(t, slot, ch)
            if ch == 0:
                edge_copy(t, slot, 1).start()
        for slot in HALO:
            if ch == 0:
                wait_edge(t, slot, 0)
            if ch == len(send) - 1:
                wait_edge(t, slot, 1)
            lo = 0 if ch == 0 else PAD + start
            hi = PAD + start + size + (2 * PAD if ch == len(send) - 1 else 0)
            widen(t, slot, lo, hi - lo)

    def transpose_rows(slots, start, end):
        def transpose_row(slot, carry):
            for b in range(NB):
                place = jnp.where(slot < 2, slot + 2, jnp.where(slot < 4, slot - 2, slot))
                row = pl.multiple_of(place * LW, LW)
                xt[b, pl.ds(row, LW), start:end] = xs[
                    b, slot, PAD + start : PAD + end, :
                ].T.astype(BF16)
                if end == cols and kcols > cols:
                    xt[b, pl.ds(row, LW), cols:kcols] = jnp.zeros((LW, kcols - cols), BF16)
            return carry

        lax.fori_loop(*slots, transpose_row, 0)

    places = {2: 0, 3: 1, 0: 2, 1: 3, 4: 4, 5: 5}
    wacc[...] = jnp.zeros(wacc.shape, F32)

    def weight_gradient(lo, hi, start, end):
        for b in range(NB):

            def weight_offset(m, carry):
                gbuf[lo * LW : hi * LW, :] = jnp.dot(
                    xt[b, lo * LW : hi * LW, start:end],
                    cw[b, m, start:end],
                    preferred_element_type=F32
                )
                sums = [wacc[k * GW : (k + 1) * GW, b * LW : (b + 1) * LW] for k in range(K)]
                for a in range(2):
                    for q in range(SMAX):
                        if not lo <= places[a + q] < hi:
                            continue
                        low = places[a + q] * LW
                        part = gbuf[low : low + GW, a * LW : (a + 1) * LW]
                        for g in range(1, PB):
                            part = jnp.where(
                                group_of == g,
                                gbuf[low + g * GW : low + (g + 1) * GW, a * LW : (a + 1) * LW],
                                part,
                            )
                        for k in range(K):
                            sums[k] = (
                                sums[k] + tab[(a * SMAX + q) * (K * WIN) + k * WIN + m] * part
                            )
                for k in range(K):
                    wacc[k * GW : (k + 1) * GW, b * LW : (b + 1) * LW] = sums[k]
                return carry

            lax.fori_loop(0, WIN, weight_offset, 0)

    transpose_rows((2, 4), 0, cols)
    weight_gradient(0, 2, 0, kcols)
    compute = computes[0]
    last = len(compute) - 1
    for ch in range(len(compute)):
        arrive(0, ch)
        start, end = compute[ch][0], compute[ch][0] + compute[ch][1]
        for slots in ((0, 2), (4, 6)):
            transpose_rows(slots, start, end)
        weight_gradient(2, 6, start, kcols if ch == last else end)
        if ch < last:
            convolve(0, ch, kf, out, 1)
    for j in range(wacc.shape[0] // LW):
        turned = wacc[j * LW : (j + 1) * LW, :].T
        for to in range(lat_n):
            place = ((to // 8 + to) % 2) * n_shares + to // 2
            wt[place * share : (place + 1) * share, j * LW : (j + 1) * LW] = turned[
                to * share : (to + 1) * share
            ]

    half_rows = C // 2

    def half_copy():
        return pltpu.make_async_remote_copy(
            src_ref=wt.at[pl.ds(pl.multiple_of(sib * half_rows, 8), half_rows)],
            dst_ref=half,
            send_sem=sum_send.at[0],
            recv_sem=sum_recv.at[0],
            device_id=(lat, sib, ens),
            device_id_type=MESH,
        )

    def share_copy(j):
        to = share_lat(j)
        return to, pltpu.make_async_remote_copy(
            src_ref=wt.at[pl.ds(pl.multiple_of(lon * half_rows + j * share, 8), share)],
            dst_ref=shares.at[jnp.where(lat < to, lat, lat - 1)],
            send_sem=share_send.at[j],
            recv_sem=share_recv,
            device_id=(to, lon, ens),
            device_id_type=MESH,
        )

    def final_copy(j):
        return pltpu.make_async_remote_copy(
            src_ref=final.at[ens],
            dst_ref=final.at[ens],
            send_sem=final_send.at[j],
            recv_sem=final_recv.at[ens],
            device_id=(lat, *partners[j]),
            device_id_type=MESH,
        )

    def sum_step(step):
        if step == 0:
            half_copy().start()
        elif step == 1:
            half_copy().wait()
            low = pl.multiple_of(lon * half_rows, 8)
            wt[pl.ds(low, half_rows), :] += half[...]
            for j in range(n_shares):
                to, copy = share_copy(j)

                @pl.when(to != lat)
                def _():
                    copy.start()

        elif step == 2:

            @pl.when(owner)
            def _():
                pltpu.make_async_copy(shares, shares, share_recv).wait()
                low = pl.multiple_of(lon * half_rows + (lat // 2) * share, 8)

                def add(j, carry):
                    return carry + shares[j]

                final[ens] = lax.fori_loop(0, lat_n - 1, add, wt[pl.ds(low, share), :])
                for j in range(3):
                    final_copy(j).start()

        else:
            for e in range(2):

                @pl.when(jnp.logical_not(jnp.logical_and(owner, ens == e)))
                def _():
                    part = final.at[e]
                    pltpu.make_async_copy(part, part, final_recv.at[e]).wait()

            total = (final[0] + final[1]) * scale
            for k in range(K):
                wout[k] = total[:, k * GW : (k + 1) * GW]

    sum_step(0)
    send_later(PACE[0])
    convolve(0, last, kf, out, 1)
    sum_step(1)
    send_later(PACE[1])
    last = len(computes[1]) - 1
    for ch in range(last + 1):
        send_later(len([c for c, _ in later if c <= ch]))
        arrive(1, ch)
        convolve(1, ch, ka, grad, -1)
        if ch == 0:
            send_later(PACE[2])
        if ch == max(last - 1, 0):
            sum_step(2)
    sum_step(3)

    for j in range(n_shares):
        to, copy = share_copy(j)

        @pl.when(to != lat)
        def _():
            copy.wait_send()

    @pl.when(owner)
    def _():
        for j in range(3):
            final_copy(j).wait_send()

    for t in range(2):
        for ch in range(len(computes[t])):
            out_copy(t, ch).wait()
        for slot in range(PANEL):
            for side in range(2):
                edge_copy(t, slot, side).wait_send()
        for a in range(2):
            for dirn in range(2):
                last_copy(t, dirn, a).wait_send()
        for ch in range(len(sends[t])):
            for dirn in range(2):
                for a in range(2):
                    for h in range(2):
                        row_copy(t, dirn, a, ch, h).wait_send()


def store(pieces, *refs):
    parts = []
    for j in range(3):
        src, dst, held = refs[j], refs[3 + j], refs[6 + j]
        size = src.shape[1] // pieces if j < 2 else src.shape[1]
        for n in range(pieces if j < 2 else 1):
            cells = (slice(None), pl.ds(n * size, size))
            parts.append(
                (
                    pltpu.make_async_copy(src.at[cells], held.at[cells], refs[9].at[j, n]),
                    pltpu.make_async_copy(held.at[cells], dst.at[cells], refs[10].at[j, n]),
                )
            )
    for bring, _ in parts:
        bring.start()
    for bring, take in parts:
        bring.wait()
        take.start()
    for _, take in parts:
        take.wait()


def shards(fields, cotangent, weights, basis_values, support, counts):
    lat_n = lax.axis_size("lat")
    cols = fields.shape[2]
    share = C // lat_n
    wcols = -(-K * GW // LW) * LW
    total = 2 * lat_n * cols * lax.axis_size("lon") * lax.axis_size("ens") * fields.shape[0]
    kcols = -(-cols // 128) * 128
    n_chunks = max(len(chunks_of(cols, width)[0]) for width in WIDTHS)
    anywhere = pl.BlockSpec(memory_space=pl.ANY)
    dma = pltpu.SemaphoreType.DMA
    out, grad, wgrad = pl.pallas_call(
        functools.partial(body, lat_n, cols, 1.0 / math.sqrt(total)),
        out_shape=(
            jax.ShapeDtypeStruct((2, cols, C), BF16),
            jax.ShapeDtypeStruct((2, cols, C), BF16),
            jax.ShapeDtypeStruct((K, share, GW), F32),
        ),
        in_specs=[pl.BlockSpec(memory_space=pltpu.HBM)] * 6,
        out_specs=(anywhere, anywhere, pl.BlockSpec(memory_space=pltpu.VMEM)),
        scratch_shapes=[
            pltpu.VMEM((PANEL, cols + 2 * PAD, C), BF16),
            pltpu.VMEM((PANEL, cols + 2 * PAD, C), BF16),
            pltpu.VMEM((NB, PANEL, cols + 2 * PAD, LW), F32),
            pltpu.VMEM((NB, PANEL, cols + 2 * PAD, LW), F32),
            pltpu.VMEM((NB, TAPS, 2 * LW), BF16),
            pltpu.VMEM((NB, TAPS, 2 * LW), BF16),
            pltpu.VMEM((NB, WIN, kcols, 2 * LW), BF16),
            pltpu.VMEM((NB, PANEL * LW, kcols), BF16),
            pltpu.VMEM((2, cols, C), BF16),
            pltpu.VMEM((2, cols, C), BF16),
            pltpu.VMEM((K, GW, C), F32),
            pltpu.VMEM((K, GW, C), F32),
            pltpu.VMEM((K, GW, C), BF16),
            pltpu.VMEM((SMAX, K, WIN, 2 * lat_n), BF16),
            pltpu.SMEM((SMAX, 2 * lat_n), jnp.int32),
            pltpu.SMEM((2 * lat_n,), jnp.int32),
            pltpu.VMEM((SMAX, K, WIN, 2 * lat_n), F32),
            pltpu.SMEM((SMAX, K, WIN, 2 * lat_n), F32),
            pltpu.VMEM((PANEL * LW, 2 * LW), F32),
            pltpu.SMEM((2 * SMAX * K * WIN,), F32),
            pltpu.VMEM((wcols, C), F32),
            pltpu.VMEM((C, wcols), F32),
            pltpu.VMEM((C // 2, wcols), F32),
            pltpu.VMEM((lat_n - 1, share, wcols), F32),
            pltpu.VMEM((2, share, wcols), F32),
            dma,
            dma((4,)),
            dma((2, n_chunks)),
            dma((2, 2)),
            dma((2, 2, 2, n_chunks, 2)),
            dma((2, PANEL, n_chunks, 2)),
            dma((2, PANEL, 2)),
            dma((2, PANEL, 2)),
            dma((2, 2, 2)),
            dma((2, PANEL)),
            dma((1,)),
            dma((1,)),
            dma((lat_n // 2,)),
            dma,
            dma((3,)),
            dma((2,)),
        ],
        compiler_params=pltpu.CompilerParams(
            collective_id=0, has_side_effects=True, vmem_limit_bytes=61 * 1024 * 1024
        ),
        name="disco",
    )(
        fields[0],
        cotangent[0],
        jnp.transpose(weights, (0, 2, 1)),
        jnp.transpose(basis_values, (1, 2, 3, 0)),
        jnp.transpose(support),
        counts,
    )
    pieces = 3
    out, grad, wgrad = pl.pallas_call(
        functools.partial(store, pieces),
        out_shape=[jax.ShapeDtypeStruct(o.shape, o.dtype) for o in (out, grad, wgrad)],
        in_specs=[anywhere] * 3,
        out_specs=[anywhere] * 3,
        scratch_shapes=[
            pltpu.VMEM(out.shape, BF16),
            pltpu.VMEM(grad.shape, BF16),
            pltpu.VMEM(wgrad.shape, F32),
            dma((3, pieces)),
            dma((3, pieces)),
        ],
        compiler_params=pltpu.CompilerParams(vmem_limit_bytes=61 * 1024 * 1024),
        name="store",
    )(out, grad, wgrad)
    return (out[None], grad[None], wgrad)


def solution(mesh):
    placed = (P("ens", "lat", "lon", None), P("ens", "lat", "lon", None), P(), P(), P(), P())
    return jax.shard_map(
        shards,
        mesh=mesh,
        in_specs=placed,
        out_specs=(
            P("ens", "lat", "lon", None),
            P("ens", "lat", "lon", None),
            P(None, "lat", None),
        ),
        check_vma=False,
    )
```

```python
import functools
import math

import jax
import jax.numpy as jnp
from jax import lax
from jax.experimental import pallas as pl
from jax.experimental.pallas import tpu as pltpu
from jax.sharding import PartitionSpec as P

MESH = pl.DeviceIdType.MESH
BF16 = jnp.bfloat16
F32 = jnp.float32

C = 256
GW = 32
K = 9
SMAX = 5
WIN = 5
PAD = 16
LW = 128
NB = C // LW
PB = LW // GW
PANEL = 6
HALO = (0, 1, 4, 5)
WIDTHS = (256, 288)
EARLY = 3
PACE = (1, 1, 1)
TAPS = PANEL * WIN * LW


def chunks_of(cols, width):
    starts = list(range(0, cols, width))
    if len(starts) > 1 and cols - starts[-1] < 32:
        starts.pop()
    compute = [(s, (starts[j + 1] if j + 1 < len(starts) else cols) - s) for j, s in enumerate(starts)]
    cuts = [0] + [s + PAD for s in starts[1:]] + [cols - PAD]
    send = [(cuts[j], cuts[j + 1] - cuts[j]) for j in range(len(starts))]
    pieces = []
    for start, size in send:
        first = -(-size // 32) * 16
        pieces.append([(start, first), (start + first, size - first)])
    return compute, pieces


def body(
    lat_n,
    cols,
    scale,
    fields,
    cot,
    weights_hbm,
    basis_hbm,
    support_hbm,
    counts_hbm,
    out_hbm,
    grad_hbm,
    wout,
    xp,
    cp,
    xs,
    cs,
    kf,
    ka,
    cw,
    xt,
    out,
    grad,
    wf,
    wa,
    weights,
    basis_in,
    support,
    counts,
    basis_wide,
    basis,
    gbuf,
    tab,
    wacc,
    wt,
    half,
    shares,
    final,
    basis_sem,
    arg_sem,
    out_sem,
    own_sem,
    row_send,
    row_recv,
    edge_send,
    edge_recv,
    last_send,
    last_recv,
    sum_send,
    sum_recv,
    share_send,
    share_recv,
    final_send,
    final_recv,
):
    computes, sends = zip(*(chunks_of(cols, width) for width in WIDTHS))
    kcols = cw.shape[2]
    lat = lax.axis_index("lat")
    lon = lax.axis_index("lon")
    ens = lax.axis_index("ens")
    sib = 1 - lon
    nlat = lat_n * 2
    top = lat == 0
    bottom = lat == lat_n - 1
    sources = (fields, cot)
    panels = (xp, cp)
    wides = (xs, cs)

    barrier = pltpu.get_barrier_semaphore()
    pl.semaphore_signal(barrier, inc=1, device_id=(lat, sib, ens), device_id_type=MESH)

    @pl.when(jnp.logical_not(top))
    def _():
        pl.semaphore_signal(barrier, inc=1, device_id=(lat - 1, lon, ens), device_id_type=MESH)

    @pl.when(jnp.logical_not(bottom))
    def _():
        pl.semaphore_signal(barrier, inc=1, device_id=(lat + 1, lon, ens), device_id_type=MESH)

    n_shares = lat_n // 2
    share = C // lat_n
    owner = lax.rem(lat // 8 + lat, 2) == lon
    partners = ((sib, ens), (lon, 1 - ens), (sib, 1 - ens))

    def share_lat(j):
        return 2 * j + lax.rem(lon + j // 4, 2)

    for to_lon, to_ens in partners[1:]:
        pl.semaphore_signal(barrier, inc=1, device_id=(lat, to_lon, to_ens), device_id_type=MESH)

    @pl.when(owner)
    def _():
        def greet(j, carry):
            pl.semaphore_signal(
                barrier, inc=1, device_id=(j + jnp.where(j < lat, 0, 1), lon, ens), device_id_type=MESH
            )
            return carry

        lax.fori_loop(0, lat_n - 1, greet, 0)

    pl.semaphore_wait(
        barrier,
        5
        + n_shares
        - jnp.where(owner, 1, 0)
        - jnp.where(top, 1, 0)
        - jnp.where(bottom, 1, 0),
    )

    def own_copy(t, a):
        return pltpu.make_async_copy(
            sources[t].at[a], panels[t].at[2 + a, pl.ds(PAD, cols)], own_sem.at[t, a]
        )

    def target(dirn, a):
        if dirn == 0:
            return (
                jnp.where(top, 0, lat - 1),
                jnp.where(top, sib, lon),
                jnp.where(top, 1 - a, 4 + a),
            )
        return (
            jnp.where(bottom, lat, lat + 1),
            jnp.where(bottom, sib, lon),
            jnp.where(bottom, 5 - a, a),
        )

    def row_copy(t, dirn, a, ch, h):
        to_lat, to_lon, slot = target(dirn, a)
        start, size = sends[t][ch][h]
        return pltpu.make_async_remote_copy(
            src_ref=sources[t].at[a, pl.ds(start, size)],
            dst_ref=panels[t].at[slot, pl.ds(PAD + start, size)],
            send_sem=row_send.at[t, dirn, a, ch, h],
            recv_sem=row_recv.at[t, slot, ch, h],
            device_id=(to_lat, to_lon, ens),
            device_id_type=MESH,
        )

    def edge_copy(t, slot, side):
        cells = pl.ds(cols - PAD if side == 0 else 0, PAD)
        if slot in (2, 3):
            src = sources[t].at[slot - 2, cells]
        else:
            src = panels[t].at[slot, pl.ds(cols if side == 0 else PAD, PAD)]
        return pltpu.make_async_remote_copy(
            src_ref=src,
            dst_ref=panels[t].at[slot, pl.ds(0 if side == 0 else PAD + cols, PAD)],
            send_sem=edge_send.at[t, slot, side],
            recv_sem=edge_recv.at[t, slot, side],
            device_id=(lat, sib, ens),
            device_id_type=MESH,
        )

    def wait_edge(t, slot, side):
        edge_copy(t, slot, side).wait_recv()

    def last_copy(t, dirn, a):
        to_lat, to_lon, slot = target(dirn, a)
        return pltpu.make_async_remote_copy(
            src_ref=sources[t].at[a, pl.ds(cols - PAD, PAD)],
            dst_ref=panels[t].at[slot, pl.ds(cols, PAD)],
            send_sem=last_send.at[t, dirn, a],
            recv_sem=last_recv.at[t, slot],
            device_id=(to_lat, to_lon, ens),
            device_id_type=MESH,
        )

    def forward_last(t):
        for slot in HALO:
            dst = panels[t].at[slot, pl.ds(cols, PAD)]
            pltpu.make_async_copy(dst, dst, last_recv.at[t, slot]).wait()
            edge_copy(t, slot, 0).start()

    def wait_row(t, slot, ch):
        for h in range(2):
            start, size = sends[t][ch][h]
            dst = panels[t].at[slot, pl.ds(PAD + start, size)]
            pltpu.make_async_copy(dst, dst, row_recv.at[t, slot, ch, h]).wait()

    def send_rows(t, ch, h):
        for a in range(2):
            for dirn in range(2):
                row_copy(t, dirn, a, ch, h).start()

    orders = [[(ch, h) for ch in range(len(send)) for h in range(2)] for send in sends]
    for t in range(2):
        for a in range(2):
            for side in range(2):
                edge_copy(t, 2 + a, side).start()
            for dirn in range(2):
                last_copy(t, dirn, a).start()
        for ch, h in orders[0] if t == 0 else orders[1][:EARLY]:
            send_rows(t, ch, h)
    small = [
        pltpu.make_async_copy(src, dst, arg_sem.at[j])
        for j, (src, dst) in enumerate(
            (
                (basis_hbm, basis_in),
                (support_hbm, support),
                (counts_hbm, counts),
                (weights_hbm, weights),
            )
        )
    ]
    for copy in small:
        copy.start()
    for t in range(2):
        for a in range(2):
            own_copy(t, a).start()
    later = orders[1][EARLY:]

    def send_later(count):
        for _ in range(min(count, len(later))):
            send_rows(1, *later.pop(0))

    small[0].wait()
    basis_wide[...] = basis_in[...].astype(F32)
    basis_copy = pltpu.make_async_copy(basis_wide, basis, basis_sem)
    basis_copy.start()
    for copy in small[1:]:
        copy.wait()
    for k in range(K):
        wide = weights[k].astype(F32)
        wf[k] = wide
        turned = wide.T
        wa[k] = jnp.concatenate([turned[g * GW : (g + 1) * GW] for g in range(C // GW)], axis=1)
    basis_copy.wait()

    group_of = lax.broadcasted_iota(jnp.int32, (GW, LW), 1) // GW

    def row_of(virtual):
        mirrored = jnp.logical_or(virtual < 0, virtual >= nlat)
        real = jnp.where(
            virtual < 0, -1 - virtual, jnp.where(virtual >= nlat, 2 * nlat - 1 - virtual, virtual)
        )
        return real, mirrored

    def coefficients(real, offset):
        first = support[0, real] - real
        slot = offset - first
        live = jnp.logical_and(slot >= 0, slot < counts[real])
        slot = jnp.minimum(jnp.maximum(slot, 0), SMAX - 1)
        gate = jnp.where(live, 1.0, 0.0).astype(F32)
        return [[basis[slot, k, m, real] * gate for m in range(WIN)] for k in range(K)]

    def spread(kref, wref, a, p, coef):
        for m0, m1 in ((0, 3), (3, 5)):
            sums = [jnp.zeros((GW, C), F32) for _ in range(m0, m1)]
            for k in range(K):
                wk = wref[k]
                for m in range(m0, m1):
                    sums[m - m0] = sums[m - m0] + coef[k][m] * wk
            for m in range(m0, m1):
                for b in range(NB):
                    part = sums[m - m0][:, b * LW : (b + 1) * LW]
                    for q in range(PB):
                        row = pl.multiple_of(p * (WIN * LW) + m * LW + q * GW, GW)
                        kref[b, pl.ds(row, GW), a * LW : (a + 1) * LW] = jnp.where(
                            group_of == q, part, 0.0
                        ).astype(BF16)

    for a in range(2):
        def forward_offset(q, carry):
            coef = coefficients(lat * 2 + a, q - 2)
            for k in range(K):
                for m in range(WIN):
                    tab[(a * SMAX + q) * (K * WIN) + k * WIN + m] = coef[k][m]
            spread(kf, wf, a, a + q, coef)
            return carry

        def adjoint_offset(q, carry):
            real, mirrored = row_of(lat * 2 - 2 + a + q)
            coef = coefficients(real, jnp.where(mirrored, q - 2, 2 - q))
            spread(ka, wa, a, a + q, coef)
            return carry

        lax.fori_loop(0, SMAX, forward_offset, 0)
        lax.fori_loop(0, SMAX, adjoint_offset, 0)
    for kref in (kf, ka):
        for b in range(NB):
            kref[b, 5 * WIN * LW :, 0:LW] = jnp.zeros((WIN * LW, LW), BF16)
            kref[b, 0 : WIN * LW, LW : 2 * LW] = jnp.zeros((WIN * LW, LW), BF16)

    def widen(t, slot, start, size):
        for b in range(NB):
            wides[t][b, slot, start : start + size, :] = panels[t][
                slot, start : start + size, b * LW : (b + 1) * LW
            ].astype(F32)

    for t in range(2):
        for a in range(2):
            own_copy(t, a).wait()
            for side in range(2):
                wait_edge(t, 2 + a, side)
            widen(t, 2 + a, 0, cols + 2 * PAD)

    def own_windows(b, carry):
        for m in range(WIN):
            for a in range(2):
                cw[b, m, 0:cols, a * LW : (a + 1) * LW] = cs[
                    b, 2 + a, PAD + 2 - m : PAD + 2 - m + cols, :
                ].astype(BF16)
            if kcols > cols:
                cw[b, m, cols:kcols, :] = jnp.zeros((kcols - cols, 2 * LW), BF16)
        return carry

    lax.fori_loop(0, NB, own_windows, 0)

    def out_copy(t, ch):
        cells = pl.ds(*computes[t][ch])
        return pltpu.make_async_copy(
            (out, grad)[t].at[:, cells], (out_hbm, grad_hbm)[t].at[:, cells], out_sem.at[t, ch]
        )

    def convolve(t, ch, kref, dest, sign):
        start, size = computes[t][ch]
        for b in range(NB):

            window = jnp.concatenate(
                [
                    wides[t][
                        b,
                        p,
                        PAD + start + sign * (m - 2) : PAD + start + sign * (m - 2) + size,
                        :,
                    ].astype(BF16)
                    for p in range(PANEL)
                    for m in range(WIN)
                ],
                axis=1,
            )
            res = jnp.dot(window, kref[b], preferred_element_type=F32)
            for a in range(2):
                dest[a, start : start + size, b * LW : (b + 1) * LW] = res[
                    :, a * LW : (a + 1) * LW
                ].astype(BF16)
        out_copy(t, ch).start()

    def arrive(t, ch):
        send = sends[t]
        start, size = send[ch][0][0], send[ch][0][1] + send[ch][1][1]
        if ch == 0:
            forward_last(t)
        for slot in HALO:
            wait_row(t, slot, ch)
            if ch == 0:
                edge_copy(t, slot, 1).start()
        for slot in HALO:
            if ch == 0:
                wait_edge(t, slot, 0)
            if ch == len(send) - 1:
                wait_edge(t, slot, 1)
            lo = 0 if ch == 0 else PAD + start
            hi = PAD + start + size + (2 * PAD if ch == len(send) - 1 else 0)
            widen(t, slot, lo, hi - lo)

    def transpose_rows(slots, start, end):
        def transpose_row(slot, carry):
            for b in range(NB):
                place = jnp.where(slot < 2, slot + 2, jnp.where(slot < 4, slot - 2, slot))
                row = pl.multiple_of(place * LW, LW)
                xt[b, pl.ds(row, LW), start:end] = xs[
                    b, slot, PAD + start : PAD + end, :
                ].T.astype(BF16)
                if end == cols and kcols > cols:
                    xt[b, pl.ds(row, LW), cols:kcols] = jnp.zeros((LW, kcols - cols), BF16)
            return carry

        lax.fori_loop(*slots, transpose_row, 0)

    places = {2: 0, 3: 1, 0: 2, 1: 3, 4: 4, 5: 5}
    wacc[...] = jnp.zeros(wacc.shape, F32)

    def weight_gradient(lo, hi, start, end):
        for b in range(NB):

            def weight_offset(m, carry):
                gbuf[lo * LW : hi * LW, :] = jnp.dot(
                    xt[b, lo * LW : hi * LW, start:end],
                    cw[b, m, start:end],
                    preferred_element_type=F32
                )
                sums = [wacc[k * GW : (k + 1) * GW, b * LW : (b + 1) * LW] for k in range(K)]
                for a in range(2):
                    for q in range(SMAX):
                        if not lo <= places[a + q] < hi:
                            continue
                        low = places[a + q] * LW
                        part = gbuf[low : low + GW, a * LW : (a + 1) * LW]
                        for g in range(1, PB):
                            part = jnp.where(
                                group_of == g,
                                gbuf[low + g * GW : low + (g + 1) * GW, a * LW : (a + 1) * LW],
                                part,
                            )
                        for k in range(K):
                            sums[k] = (
                                sums[k] + tab[(a * SMAX + q) * (K * WIN) + k * WIN + m] * part
                            )
                for k in range(K):
                    wacc[k * GW : (k + 1) * GW, b * LW : (b + 1) * LW] = sums[k]
                return carry

            lax.fori_loop(0, WIN, weight_offset, 0)

    transpose_rows((2, 4), 0, cols)
    weight_gradient(0, 2, 0, kcols)
    compute = computes[0]
    last = len(compute) - 1
    for ch in range(len(compute)):
        arrive(0, ch)
        start, end = compute[ch][0], compute[ch][0] + compute[ch][1]
        for slots in ((0, 2), (4, 6)):
            transpose_rows(slots, start, end)
        weight_gradient(2, 6, start, kcols if ch == last else end)
        if ch < last:
            convolve(0, ch, kf, out, 1)
    for j in range(wacc.shape[0] // LW):
        turned = wacc[j * LW : (j + 1) * LW, :].T
        for to in range(lat_n):
            place = ((to // 8 + to) % 2) * n_shares + to // 2
            wt[place * share : (place + 1) * share, j * LW : (j + 1) * LW] = turned[
                to * share : (to + 1) * share
            ]

    half_rows = C // 2

    def half_copy():
        return pltpu.make_async_remote_copy(
            src_ref=wt.at[pl.ds(pl.multiple_of(sib * half_rows, 8), half_rows)],
            dst_ref=half,
            send_sem=sum_send.at[0],
            recv_sem=sum_recv.at[0],
            device_id=(lat, sib, ens),
            device_id_type=MESH,
        )

    def share_copy(j):
        to = share_lat(j)
        return to, pltpu.make_async_remote_copy(
            src_ref=wt.at[pl.ds(pl.multiple_of(lon * half_rows + j * share, 8), share)],
            dst_ref=shares.at[jnp.where(lat < to, lat, lat - 1)],
            send_sem=share_send.at[j],
            recv_sem=share_recv,
            device_id=(to, lon, ens),
            device_id_type=MESH,
        )

    def final_copy(j):
        return pltpu.make_async_remote_copy(
            src_ref=final.at[ens],
            dst_ref=final.at[ens],
            send_sem=final_send.at[j],
            recv_sem=final_recv.at[ens],
            device_id=(lat, *partners[j]),
            device_id_type=MESH,
        )

    def sum_step(step):
        if step == 0:
            half_copy().start()
        elif step == 1:
            half_copy().wait()
            low = pl.multiple_of(lon * half_rows, 8)
            wt[pl.ds(low, half_rows), :] += half[...]
            for j in range(n_shares):
                to, copy = share_copy(lax.rem(j + lat // 2, n_shares))

                @pl.when(to != lat)
                def _():
                    copy.start()

        elif step == 2:

            @pl.when(owner)
            def _():
                pltpu.make_async_copy(shares, shares, share_recv).wait()
                low = pl.multiple_of(lon * half_rows + (lat // 2) * share, 8)

                def add(j, carry):
                    return carry + shares[j]

                final[ens] = lax.fori_loop(0, lat_n - 1, add, wt[pl.ds(low, share), :])
                for j in range(3):
                    final_copy(j).start()

        else:
            for e in range(2):

                @pl.when(jnp.logical_not(jnp.logical_and(owner, ens == e)))
                def _():
                    part = final.at[e]
                    pltpu.make_async_copy(part, part, final_recv.at[e]).wait()

            total = (final[0] + final[1]) * scale
            for k in range(K):
                wout[k] = total[:, k * GW : (k + 1) * GW]

    sum_step(0)
    sum_step(1)
    send_later(PACE[0])
    convolve(0, last, kf, out, 1)
    send_later(PACE[1])
    last = len(computes[1]) - 1
    for ch in range(last + 1):
        send_later(len([c for c, _ in later if c <= ch]))
        arrive(1, ch)
        convolve(1, ch, ka, grad, -1)
        if ch == 0:
            send_later(PACE[2])
        if ch == max(last - 1, 0):
            sum_step(2)
    sum_step(3)

    for j in range(n_shares):
        to, copy = share_copy(j)

        @pl.when(to != lat)
        def _():
            copy.wait_send()

    @pl.when(owner)
    def _():
        for j in range(3):
            final_copy(j).wait_send()

    for t in range(2):
        for ch in range(len(computes[t])):
            out_copy(t, ch).wait()
        for slot in range(PANEL):
            for side in range(2):
                edge_copy(t, slot, side).wait_send()
        for a in range(2):
            for dirn in range(2):
                last_copy(t, dirn, a).wait_send()
        for ch in range(len(sends[t])):
            for dirn in range(2):
                for a in range(2):
                    for h in range(2):
                        row_copy(t, dirn, a, ch, h).wait_send()


def store(pieces, *refs):
    parts = []
    for j in range(3):
        src, dst, held = refs[j], refs[3 + j], refs[6 + j]
        size = src.shape[1] // pieces if j < 2 else src.shape[1]
        for n in range(pieces if j < 2 else 1):
            cells = (slice(None), pl.ds(n * size, size))
            parts.append(
                (
                    pltpu.make_async_copy(src.at[cells], held.at[cells], refs[9].at[j, n]),
                    pltpu.make_async_copy(held.at[cells], dst.at[cells], refs[10].at[j, n]),
                )
            )
    for bring, _ in parts:
        bring.start()
    for bring, take in parts:
        bring.wait()
        take.start()
    for _, take in parts:
        take.wait()


def shards(fields, cotangent, weights, basis_values, support, counts):
    lat_n = lax.axis_size("lat")
    cols = fields.shape[2]
    share = C // lat_n
    wcols = -(-K * GW // LW) * LW
    total = 2 * lat_n * cols * lax.axis_size("lon") * lax.axis_size("ens") * fields.shape[0]
    kcols = -(-cols // 128) * 128
    n_chunks = max(len(chunks_of(cols, width)[0]) for width in WIDTHS)
    anywhere = pl.BlockSpec(memory_space=pl.ANY)
    dma = pltpu.SemaphoreType.DMA
    out, grad, wgrad = pl.pallas_call(
        functools.partial(body, lat_n, cols, 1.0 / math.sqrt(total)),
        out_shape=(
            jax.ShapeDtypeStruct((2, cols, C), BF16),
            jax.ShapeDtypeStruct((2, cols, C), BF16),
            jax.ShapeDtypeStruct((K, share, GW), F32),
        ),
        in_specs=[pl.BlockSpec(memory_space=pltpu.HBM)] * 6,
        out_specs=(anywhere, anywhere, pl.BlockSpec(memory_space=pltpu.VMEM)),
        scratch_shapes=[
            pltpu.VMEM((PANEL, cols + 2 * PAD, C), BF16),
            pltpu.VMEM((PANEL, cols + 2 * PAD, C), BF16),
            pltpu.VMEM((NB, PANEL, cols + 2 * PAD, LW), F32),
            pltpu.VMEM((NB, PANEL, cols + 2 * PAD, LW), F32),
            pltpu.VMEM((NB, TAPS, 2 * LW), BF16),
            pltpu.VMEM((NB, TAPS, 2 * LW), BF16),
            pltpu.VMEM((NB, WIN, kcols, 2 * LW), BF16),
            pltpu.VMEM((NB, PANEL * LW, kcols), BF16),
            pltpu.VMEM((2, cols, C), BF16),
            pltpu.VMEM((2, cols, C), BF16),
            pltpu.VMEM((K, GW, C), F32),
            pltpu.VMEM((K, GW, C), F32),
            pltpu.VMEM((K, GW, C), BF16),
            pltpu.VMEM((SMAX, K, WIN, 2 * lat_n), BF16),
            pltpu.SMEM((SMAX, 2 * lat_n), jnp.int32),
            pltpu.SMEM((2 * lat_n,), jnp.int32),
            pltpu.VMEM((SMAX, K, WIN, 2 * lat_n), F32),
            pltpu.SMEM((SMAX, K, WIN, 2 * lat_n), F32),
            pltpu.VMEM((PANEL * LW, 2 * LW), F32),
            pltpu.SMEM((2 * SMAX * K * WIN,), F32),
            pltpu.VMEM((wcols, C), F32),
            pltpu.VMEM((C, wcols), F32),
            pltpu.VMEM((C // 2, wcols), F32),
            pltpu.VMEM((lat_n - 1, share, wcols), F32),
            pltpu.VMEM((2, share, wcols), F32),
            dma,
            dma((4,)),
            dma((2, n_chunks)),
            dma((2, 2)),
            dma((2, 2, 2, n_chunks, 2)),
            dma((2, PANEL, n_chunks, 2)),
            dma((2, PANEL, 2)),
            dma((2, PANEL, 2)),
            dma((2, 2, 2)),
            dma((2, PANEL)),
            dma((1,)),
            dma((1,)),
            dma((lat_n // 2,)),
            dma,
            dma((3,)),
            dma((2,)),
        ],
        compiler_params=pltpu.CompilerParams(
            collective_id=0, has_side_effects=True, vmem_limit_bytes=61 * 1024 * 1024
        ),
        name="disco",
    )(
        fields[0],
        cotangent[0],
        jnp.transpose(weights, (0, 2, 1)),
        jnp.transpose(basis_values, (1, 2, 3, 0)),
        jnp.transpose(support),
        counts,
    )
    pieces = 3
    out, grad, wgrad = pl.pallas_call(
        functools.partial(store, pieces),
        out_shape=[jax.ShapeDtypeStruct(o.shape, o.dtype) for o in (out, grad, wgrad)],
        in_specs=[anywhere] * 3,
        out_specs=[anywhere] * 3,
        scratch_shapes=[
            pltpu.VMEM(out.shape, BF16),
            pltpu.VMEM(grad.shape, BF16),
            pltpu.VMEM(wgrad.shape, F32),
            dma((3, pieces)),
            dma((3, pieces)),
        ],
        compiler_params=pltpu.CompilerParams(vmem_limit_bytes=61 * 1024 * 1024),
        name="store",
    )(out, grad, wgrad)
    return (out[None], grad[None], wgrad)


def solution(mesh):
    placed = (P("ens", "lat", "lon", None), P("ens", "lat", "lon", None), P(), P(), P(), P())
    return jax.shard_map(
        shards,
        mesh=mesh,
        in_specs=placed,
        out_specs=(
            P("ens", "lat", "lon", None),
            P("ens", "lat", "lon", None),
            P(None, "lat", None),
        ),
        check_vma=False,
    )
```

```python
import functools
import math

import jax
import jax.numpy as jnp
from jax import lax
from jax.experimental import pallas as pl
from jax.experimental.pallas import tpu as pltpu
from jax.sharding import PartitionSpec as P

MESH = pl.DeviceIdType.MESH
BF16 = jnp.bfloat16
F32 = jnp.float32

C = 256
GW = 32
K = 9
SMAX = 5
WIN = 5
PAD = 16
LW = 128
NB = C // LW
PB = LW // GW
PANEL = 6
HALO = (0, 1, 4, 5)
WIDTHS = (256, 304)
EARLY = 3
PACE = (1, 1, 1)
TAPS = PANEL * WIN * LW


def chunks_of(cols, width):
    starts = list(range(0, cols, width))
    if len(starts) > 1 and cols - starts[-1] < 32:
        starts.pop()
    compute = [(s, (starts[j + 1] if j + 1 < len(starts) else cols) - s) for j, s in enumerate(starts)]
    cuts = [0] + [s + PAD for s in starts[1:]] + [cols - PAD]
    send = [(cuts[j], cuts[j + 1] - cuts[j]) for j in range(len(starts))]
    pieces = []
    for start, size in send:
        first = -(-size // 32) * 16
        pieces.append([(start, first), (start + first, size - first)])
    return compute, pieces


def body(
    lat_n,
    cols,
    scale,
    fields,
    cot,
    weights_hbm,
    basis_hbm,
    support_hbm,
    counts_hbm,
    out_hbm,
    grad_hbm,
    wout,
    xp,
    cp,
    xs,
    cs,
    kf,
    ka,
    cw,
    xt,
    out,
    grad,
    wf,
    wa,
    weights,
    basis_in,
    support,
    counts,
    basis_wide,
    basis,
    gbuf,
    tab,
    wacc,
    wt,
    half,
    shares,
    final,
    basis_sem,
    arg_sem,
    out_sem,
    own_sem,
    row_send,
    row_recv,
    edge_send,
    edge_recv,
    last_send,
    last_recv,
    sum_send,
    sum_recv,
    share_send,
    share_recv,
    final_send,
    final_recv,
):
    computes, sends = zip(*(chunks_of(cols, width) for width in WIDTHS))
    kcols = cw.shape[2]
    lat = lax.axis_index("lat")
    lon = lax.axis_index("lon")
    ens = lax.axis_index("ens")
    sib = 1 - lon
    nlat = lat_n * 2
    top = lat == 0
    bottom = lat == lat_n - 1
    sources = (fields, cot)
    panels = (xp, cp)
    wides = (xs, cs)

    barrier = pltpu.get_barrier_semaphore()
    pl.semaphore_signal(barrier, inc=1, device_id=(lat, sib, ens), device_id_type=MESH)

    @pl.when(jnp.logical_not(top))
    def _():
        pl.semaphore_signal(barrier, inc=1, device_id=(lat - 1, lon, ens), device_id_type=MESH)

    @pl.when(jnp.logical_not(bottom))
    def _():
        pl.semaphore_signal(barrier, inc=1, device_id=(lat + 1, lon, ens), device_id_type=MESH)

    n_shares = lat_n // 2
    share = C // lat_n
    owner = lax.rem(lat // 8 + lat, 2) == lon
    partners = ((sib, ens), (lon, 1 - ens), (sib, 1 - ens))

    def share_lat(j):
        return 2 * j + lax.rem(lon + j // 4, 2)

    for to_lon, to_ens in partners[1:]:
        pl.semaphore_signal(barrier, inc=1, device_id=(lat, to_lon, to_ens), device_id_type=MESH)

    @pl.when(owner)
    def _():
        def greet(j, carry):
            pl.semaphore_signal(
                barrier, inc=1, device_id=(j + jnp.where(j < lat, 0, 1), lon, ens), device_id_type=MESH
            )
            return carry

        lax.fori_loop(0, lat_n - 1, greet, 0)

    pl.semaphore_wait(
        barrier,
        5
        + n_shares
        - jnp.where(owner, 1, 0)
        - jnp.where(top, 1, 0)
        - jnp.where(bottom, 1, 0),
    )

    def own_copy(t, a):
        return pltpu.make_async_copy(
            sources[t].at[a], panels[t].at[2 + a, pl.ds(PAD, cols)], own_sem.at[t, a]
        )

    def target(dirn, a):
        if dirn == 0:
            return (
                jnp.where(top, 0, lat - 1),
                jnp.where(top, sib, lon),
                jnp.where(top, 1 - a, 4 + a),
            )
        return (
            jnp.where(bottom, lat, lat + 1),
            jnp.where(bottom, sib, lon),
            jnp.where(bottom, 5 - a, a),
        )

    def row_copy(t, dirn, a, ch, h):
        to_lat, to_lon, slot = target(dirn, a)
        start, size = sends[t][ch][h]
        return pltpu.make_async_remote_copy(
            src_ref=sources[t].at[a, pl.ds(start, size)],
            dst_ref=panels[t].at[slot, pl.ds(PAD + start, size)],
            send_sem=row_send.at[t, dirn, a, ch, h],
            recv_sem=row_recv.at[t, slot, ch, h],
            device_id=(to_lat, to_lon, ens),
            device_id_type=MESH,
        )

    def edge_copy(t, slot, side):
        cells = pl.ds(cols - PAD if side == 0 else 0, PAD)
        if slot in (2, 3):
            src = sources[t].at[slot - 2, cells]
        else:
            src = panels[t].at[slot, pl.ds(cols if side == 0 else PAD, PAD)]
        return pltpu.make_async_remote_copy(
            src_ref=src,
            dst_ref=panels[t].at[slot, pl.ds(0 if side == 0 else PAD + cols, PAD)],
            send_sem=edge_send.at[t, slot, side],
            recv_sem=edge_recv.at[t, slot, side],
            device_id=(lat, sib, ens),
            device_id_type=MESH,
        )

    def wait_edge(t, slot, side):
        edge_copy(t, slot, side).wait_recv()

    def last_copy(t, dirn, a):
        to_lat, to_lon, slot = target(dirn, a)
        return pltpu.make_async_remote_copy(
            src_ref=sources[t].at[a, pl.ds(cols - PAD, PAD)],
            dst_ref=panels[t].at[slot, pl.ds(cols, PAD)],
            send_sem=last_send.at[t, dirn, a],
            recv_sem=last_recv.at[t, slot],
            device_id=(to_lat, to_lon, ens),
            device_id_type=MESH,
        )

    def forward_last(t):
        for slot in HALO:
            dst = panels[t].at[slot, pl.ds(cols, PAD)]
            pltpu.make_async_copy(dst, dst, last_recv.at[t, slot]).wait()
            edge_copy(t, slot, 0).start()

    def wait_row(t, slot, ch):
        for h in range(2):
            start, size = sends[t][ch][h]
            dst = panels[t].at[slot, pl.ds(PAD + start, size)]
            pltpu.make_async_copy(dst, dst, row_recv.at[t, slot, ch, h]).wait()

    def send_rows(t, ch, h):
        for a in range(2):
            for dirn in range(2):
                row_copy(t, dirn, a, ch, h).start()

    orders = [[(ch, h) for ch in range(len(send)) for h in range(2)] for send in sends]
    for t in range(2):
        for a in range(2):
            for side in range(2):
                edge_copy(t, 2 + a, side).start()
            for dirn in range(2):
                last_copy(t, dirn, a).start()
        for ch, h in orders[0] if t == 0 else orders[1][:EARLY]:
            send_rows(t, ch, h)
    small = [
        pltpu.make_async_copy(src, dst, arg_sem.at[j])
        for j, (src, dst) in enumerate(
            (
                (basis_hbm, basis_in),
                (support_hbm, support),
                (counts_hbm, counts),
                (weights_hbm, weights),
            )
        )
    ]
    for copy in small:
        copy.start()
    for t in range(2):
        for a in range(2):
            own_copy(t, a).start()
    later = orders[1][EARLY:]

    def send_later(count):
        for _ in range(min(count, len(later))):
            send_rows(1, *later.pop(0))

    small[0].wait()
    basis_wide[...] = basis_in[...].astype(F32)
    basis_copy = pltpu.make_async_copy(basis_wide, basis, basis_sem)
    basis_copy.start()
    for copy in small[1:]:
        copy.wait()
    for k in range(K):
        wide = weights[k].astype(F32)
        wf[k] = wide
        turned = wide.T
        wa[k] = jnp.concatenate([turned[g * GW : (g + 1) * GW] for g in range(C // GW)], axis=1)
    basis_copy.wait()

    group_of = lax.broadcasted_iota(jnp.int32, (GW, LW), 1) // GW

    def row_of(virtual):
        mirrored = jnp.logical_or(virtual < 0, virtual >= nlat)
        real = jnp.where(
            virtual < 0, -1 - virtual, jnp.where(virtual >= nlat, 2 * nlat - 1 - virtual, virtual)
        )
        return real, mirrored

    def coefficients(real, offset):
        first = support[0, real] - real
        slot = offset - first
        live = jnp.logical_and(slot >= 0, slot < counts[real])
        slot = jnp.minimum(jnp.maximum(slot, 0), SMAX - 1)
        gate = jnp.where(live, 1.0, 0.0).astype(F32)
        return [[basis[slot, k, m, real] * gate for m in range(WIN)] for k in range(K)]

    def spread(kref, wref, a, p, coef):
        for m0, m1 in ((0, 3), (3, 5)):
            sums = [jnp.zeros((GW, C), F32) for _ in range(m0, m1)]
            for k in range(K):
                wk = wref[k]
                for m in range(m0, m1):
                    sums[m - m0] = sums[m - m0] + coef[k][m] * wk
            for m in range(m0, m1):
                for b in range(NB):
                    part = sums[m - m0][:, b * LW : (b + 1) * LW]
                    for q in range(PB):
                        row = pl.multiple_of(p * (WIN * LW) + m * LW + q * GW, GW)
                        kref[b, pl.ds(row, GW), a * LW : (a + 1) * LW] = jnp.where(
                            group_of == q, part, 0.0
                        ).astype(BF16)

    for a in range(2):
        def forward_offset(q, carry):
            coef = coefficients(lat * 2 + a, q - 2)
            for k in range(K):
                for m in range(WIN):
                    tab[(a * SMAX + q) * (K * WIN) + k * WIN + m] = coef[k][m]
            spread(kf, wf, a, a + q, coef)
            return carry

        def adjoint_offset(q, carry):
            real, mirrored = row_of(lat * 2 - 2 + a + q)
            coef = coefficients(real, jnp.where(mirrored, q - 2, 2 - q))
            spread(ka, wa, a, a + q, coef)
            return carry

        lax.fori_loop(0, SMAX, forward_offset, 0)
        lax.fori_loop(0, SMAX, adjoint_offset, 0)
    for kref in (kf, ka):
        for b in range(NB):
            kref[b, 5 * WIN * LW :, 0:LW] = jnp.zeros((WIN * LW, LW), BF16)
            kref[b, 0 : WIN * LW, LW : 2 * LW] = jnp.zeros((WIN * LW, LW), BF16)

    def widen(t, slot, start, size):
        for b in range(NB):
            wides[t][b, slot, start : start + size, :] = panels[t][
                slot, start : start + size, b * LW : (b + 1) * LW
            ].astype(F32)

    for t in range(2):
        for a in range(2):
            own_copy(t, a).wait()
            for side in range(2):
                wait_edge(t, 2 + a, side)
            widen(t, 2 + a, 0, cols + 2 * PAD)

    def own_windows(b, carry):
        for m in range(WIN):
            for a in range(2):
                cw[b, m, 0:cols, a * LW : (a + 1) * LW] = cs[
                    b, 2 + a, PAD + 2 - m : PAD + 2 - m + cols, :
                ].astype(BF16)
            if kcols > cols:
                cw[b, m, cols:kcols, :] = jnp.zeros((kcols - cols, 2 * LW), BF16)
        return carry

    lax.fori_loop(0, NB, own_windows, 0)

    def out_copy(t, ch):
        cells = pl.ds(*computes[t][ch])
        return pltpu.make_async_copy(
            (out, grad)[t].at[:, cells], (out_hbm, grad_hbm)[t].at[:, cells], out_sem.at[t, ch]
        )

    def convolve(t, ch, kref, dest, sign):
        start, size = computes[t][ch]
        for b in range(NB):

            window = jnp.concatenate(
                [
                    wides[t][
                        b,
                        p,
                        PAD + start + sign * (m - 2) : PAD + start + sign * (m - 2) + size,
                        :,
                    ].astype(BF16)
                    for p in range(PANEL)
                    for m in range(WIN)
                ],
                axis=1,
            )
            res = jnp.dot(window, kref[b], preferred_element_type=F32)
            for a in range(2):
                dest[a, start : start + size, b * LW : (b + 1) * LW] = res[
                    :, a * LW : (a + 1) * LW
                ].astype(BF16)
        out_copy(t, ch).start()

    def arrive(t, ch):
        send = sends[t]
        start, size = send[ch][0][0], send[ch][0][1] + send[ch][1][1]
        if ch == 0:
            forward_last(t)
        for slot in HALO:
            wait_row(t, slot, ch)
            if ch == 0:
                edge_copy(t, slot, 1).start()
        for slot in HALO:
            if ch == 0:
                wait_edge(t, slot, 0)
            if ch == len(send) - 1:
                wait_edge(t, slot, 1)
            lo = 0 if ch == 0 else PAD + start
            hi = PAD + start + size + (2 * PAD if ch == len(send) - 1 else 0)
            widen(t, slot, lo, hi - lo)

    def transpose_rows(slots, start, end):
        def transpose_row(slot, carry):
            for b in range(NB):
                place = jnp.where(slot < 2, slot + 2, jnp.where(slot < 4, slot - 2, slot))
                row = pl.multiple_of(place * LW, LW)
                xt[b, pl.ds(row, LW), start:end] = xs[
                    b, slot, PAD + start : PAD + end, :
                ].T.astype(BF16)
                if end == cols and kcols > cols:
                    xt[b, pl.ds(row, LW), cols:kcols] = jnp.zeros((LW, kcols - cols), BF16)
            return carry

        lax.fori_loop(*slots, transpose_row, 0)

    places = {2: 0, 3: 1, 0: 2, 1: 3, 4: 4, 5: 5}
    wacc[...] = jnp.zeros(wacc.shape, F32)

    def weight_gradient(lo, hi, start, end):
        for b in range(NB):

            def weight_offset(m, carry):
                gbuf[lo * LW : hi * LW, :] = jnp.dot(
                    xt[b, lo * LW : hi * LW, start:end],
                    cw[b, m, start:end],
                    preferred_element_type=F32
                )
                sums = [wacc[k * GW : (k + 1) * GW, b * LW : (b + 1) * LW] for k in range(K)]
                for a in range(2):
                    for q in range(SMAX):
                        if not lo <= places[a + q] < hi:
                            continue
                        low = places[a + q] * LW
                        part = gbuf[low : low + GW, a * LW : (a + 1) * LW]
                        for g in range(1, PB):
                            part = jnp.where(
                                group_of == g,
                                gbuf[low + g * GW : low + (g + 1) * GW, a * LW : (a + 1) * LW],
                                part,
                            )
                        for k in range(K):
                            sums[k] = (
                                sums[k] + tab[(a * SMAX + q) * (K * WIN) + k * WIN + m] * part
                            )
                for k in range(K):
                    wacc[k * GW : (k + 1) * GW, b * LW : (b + 1) * LW] = sums[k]
                return carry

            lax.fori_loop(0, WIN, weight_offset, 0)

    transpose_rows((2, 4), 0, cols)
    weight_gradient(0, 2, 0, kcols)
    compute = computes[0]
    last = len(compute) - 1
    for ch in range(len(compute)):
        arrive(0, ch)
        start, end = compute[ch][0], compute[ch][0] + compute[ch][1]
        for slots in ((0, 2), (4, 6)):
            transpose_rows(slots, start, end)
        weight_gradient(2, 6, start, kcols if ch == last else end)
        if ch < last:
            convolve(0, ch, kf, out, 1)
    for j in range(wacc.shape[0] // LW):
        turned = wacc[j * LW : (j + 1) * LW, :].T
        for to in range(lat_n):
            place = ((to // 8 + to) % 2) * n_shares + to // 2
            wt[place * share : (place + 1) * share, j * LW : (j + 1) * LW] = turned[
                to * share : (to + 1) * share
            ]

    half_rows = C // 2

    def half_copy():
        return pltpu.make_async_remote_copy(
            src_ref=wt.at[pl.ds(pl.multiple_of(sib * half_rows, 8), half_rows)],
            dst_ref=half,
            send_sem=sum_send.at[0],
            recv_sem=sum_recv.at[0],
            device_id=(lat, sib, ens),
            device_id_type=MESH,
        )

    def share_copy(j):
        to = share_lat(j)
        return to, pltpu.make_async_remote_copy(
            src_ref=wt.at[pl.ds(pl.multiple_of(lon * half_rows + j * share, 8), share)],
            dst_ref=shares.at[jnp.where(lat < to, lat, lat - 1)],
            send_sem=share_send.at[j],
            recv_sem=share_recv,
            device_id=(to, lon, ens),
            device_id_type=MESH,
        )

    def final_copy(j):
        return pltpu.make_async_remote_copy(
            src_ref=final.at[ens],
            dst_ref=final.at[ens],
            send_sem=final_send.at[j],
            recv_sem=final_recv.at[ens],
            device_id=(lat, *partners[j]),
            device_id_type=MESH,
        )

    def sum_step(step):
        if step == 0:
            half_copy().start()
        elif step == 1:
            half_copy().wait()
            low = pl.multiple_of(lon * half_rows, 8)
            wt[pl.ds(low, half_rows), :] += half[...]
            for j in range(n_shares):
                to, copy = share_copy(j)

                @pl.when(to != lat)
                def _():
                    copy.start()

        elif step == 2:

            @pl.when(owner)
            def _():
                pltpu.make_async_copy(shares, shares, share_recv).wait()
                low = pl.multiple_of(lon * half_rows + (lat // 2) * share, 8)

                def add(j, carry):
                    return carry + shares[j]

                final[ens] = lax.fori_loop(0, lat_n - 1, add, wt[pl.ds(low, share), :])
                for j in range(3):
                    final_copy(j).start()

        else:
            for e in range(2):

                @pl.when(jnp.logical_not(jnp.logical_and(owner, ens == e)))
                def _():
                    part = final.at[e]
                    pltpu.make_async_copy(part, part, final_recv.at[e]).wait()

            total = (final[0] + final[1]) * scale
            for k in range(K):
                wout[k] = total[:, k * GW : (k + 1) * GW]

    sum_step(0)
    sum_step(1)
    send_later(PACE[0])
    convolve(0, last, kf, out, 1)
    send_later(PACE[1])
    last = len(computes[1]) - 1
    for ch in range(last + 1):
        send_later(len([c for c, _ in later if c <= ch]))
        arrive(1, ch)
        convolve(1, ch, ka, grad, -1)
        if ch == 0:
            send_later(PACE[2])
        if ch == max(last - 1, 0):
            sum_step(2)
    sum_step(3)

    for j in range(n_shares):
        to, copy = share_copy(j)

        @pl.when(to != lat)
        def _():
            copy.wait_send()

    @pl.when(owner)
    def _():
        for j in range(3):
            final_copy(j).wait_send()

    for t in range(2):
        for ch in range(len(computes[t])):
            out_copy(t, ch).wait()
        for slot in range(PANEL):
            for side in range(2):
                edge_copy(t, slot, side).wait_send()
        for a in range(2):
            for dirn in range(2):
                last_copy(t, dirn, a).wait_send()
        for ch in range(len(sends[t])):
            for dirn in range(2):
                for a in range(2):
                    for h in range(2):
                        row_copy(t, dirn, a, ch, h).wait_send()


def store(pieces, *refs):
    parts = []
    for j in range(3):
        src, dst, held = refs[j], refs[3 + j], refs[6 + j]
        size = src.shape[1] // pieces if j < 2 else src.shape[1]
        for n in range(pieces if j < 2 else 1):
            cells = (slice(None), pl.ds(n * size, size))
            parts.append(
                (
                    pltpu.make_async_copy(src.at[cells], held.at[cells], refs[9].at[j, n]),
                    pltpu.make_async_copy(held.at[cells], dst.at[cells], refs[10].at[j, n]),
                )
            )
    for bring, _ in parts:
        bring.start()
    for bring, take in parts:
        bring.wait()
        take.start()
    for _, take in parts:
        take.wait()


def shards(fields, cotangent, weights, basis_values, support, counts):
    lat_n = lax.axis_size("lat")
    cols = fields.shape[2]
    share = C // lat_n
    wcols = -(-K * GW // LW) * LW
    total = 2 * lat_n * cols * lax.axis_size("lon") * lax.axis_size("ens") * fields.shape[0]
    kcols = -(-cols // 128) * 128
    n_chunks = max(len(chunks_of(cols, width)[0]) for width in WIDTHS)
    anywhere = pl.BlockSpec(memory_space=pl.ANY)
    dma = pltpu.SemaphoreType.DMA
    out, grad, wgrad = pl.pallas_call(
        functools.partial(body, lat_n, cols, 1.0 / math.sqrt(total)),
        out_shape=(
            jax.ShapeDtypeStruct((2, cols, C), BF16),
            jax.ShapeDtypeStruct((2, cols, C), BF16),
            jax.ShapeDtypeStruct((K, share, GW), F32),
        ),
        in_specs=[pl.BlockSpec(memory_space=pltpu.HBM)] * 6,
        out_specs=(anywhere, anywhere, pl.BlockSpec(memory_space=pltpu.VMEM)),
        scratch_shapes=[
            pltpu.VMEM((PANEL, cols + 2 * PAD, C), BF16),
            pltpu.VMEM((PANEL, cols + 2 * PAD, C), BF16),
            pltpu.VMEM((NB, PANEL, cols + 2 * PAD, LW), F32),
            pltpu.VMEM((NB, PANEL, cols + 2 * PAD, LW), F32),
            pltpu.VMEM((NB, TAPS, 2 * LW), BF16),
            pltpu.VMEM((NB, TAPS, 2 * LW), BF16),
            pltpu.VMEM((NB, WIN, kcols, 2 * LW), BF16),
            pltpu.VMEM((NB, PANEL * LW, kcols), BF16),
            pltpu.VMEM((2, cols, C), BF16),
            pltpu.VMEM((2, cols, C), BF16),
            pltpu.VMEM((K, GW, C), F32),
            pltpu.VMEM((K, GW, C), F32),
            pltpu.VMEM((K, GW, C), BF16),
            pltpu.VMEM((SMAX, K, WIN, 2 * lat_n), BF16),
            pltpu.SMEM((SMAX, 2 * lat_n), jnp.int32),
            pltpu.SMEM((2 * lat_n,), jnp.int32),
            pltpu.VMEM((SMAX, K, WIN, 2 * lat_n), F32),
            pltpu.SMEM((SMAX, K, WIN, 2 * lat_n), F32),
            pltpu.VMEM((PANEL * LW, 2 * LW), F32),
            pltpu.SMEM((2 * SMAX * K * WIN,), F32),
            pltpu.VMEM((wcols, C), F32),
            pltpu.VMEM((C, wcols), F32),
            pltpu.VMEM((C // 2, wcols), F32),
            pltpu.VMEM((lat_n - 1, share, wcols), F32),
            pltpu.VMEM((2, share, wcols), F32),
            dma,
            dma((4,)),
            dma((2, n_chunks)),
            dma((2, 2)),
            dma((2, 2, 2, n_chunks, 2)),
            dma((2, PANEL, n_chunks, 2)),
            dma((2, PANEL, 2)),
            dma((2, PANEL, 2)),
            dma((2, 2, 2)),
            dma((2, PANEL)),
            dma((1,)),
            dma((1,)),
            dma((lat_n // 2,)),
            dma,
            dma((3,)),
            dma((2,)),
        ],
        compiler_params=pltpu.CompilerParams(
            collective_id=0, has_side_effects=True, vmem_limit_bytes=61 * 1024 * 1024
        ),
        name="disco",
    )(
        fields[0],
        cotangent[0],
        jnp.transpose(weights, (0, 2, 1)),
        jnp.transpose(basis_values, (1, 2, 3, 0)),
        jnp.transpose(support),
        counts,
    )
    pieces = 3
    out, grad, wgrad = pl.pallas_call(
        functools.partial(store, pieces),
        out_shape=[jax.ShapeDtypeStruct(o.shape, o.dtype) for o in (out, grad, wgrad)],
        in_specs=[anywhere] * 3,
        out_specs=[anywhere] * 3,
        scratch_shapes=[
            pltpu.VMEM(out.shape, BF16),
            pltpu.VMEM(grad.shape, BF16),
            pltpu.VMEM(wgrad.shape, F32),
            dma((3, pieces)),
            dma((3, pieces)),
        ],
        compiler_params=pltpu.CompilerParams(vmem_limit_bytes=61 * 1024 * 1024),
        name="store",
    )(out, grad, wgrad)
    return (out[None], grad[None], wgrad)


def solution(mesh):
    placed = (P("ens", "lat", "lon", None), P("ens", "lat", "lon", None), P(), P(), P(), P())
    return jax.shard_map(
        shards,
        mesh=mesh,
        in_specs=placed,
        out_specs=(
            P("ens", "lat", "lon", None),
            P("ens", "lat", "lon", None),
            P(None, "lat", None),
        ),
        check_vma=False,
    )
```
